32 devices in a mesh: gy: 8 (over y, x, core), gz: 4 (over z).
Axes of the slice: x: 2, y: 2, z: 4, core: 2. Of those that a mesh axis runs over, the one named last changes fastest.
Arguments:
- efield_check: bfloat16 [3, 256, 8, 1024], P(None, 'gy', None, 'gz'), may hold values from -6 to 6
- hfield_check: bfloat16 [3, 256, 8, 1024], P(None, 'gy', None, 'gz'), may hold values from -6 to 6
- polar_check: bfloat16 [3, 256, 8, 1024], P(None, 'gy', None, 'gz'), may hold values from -4 to 4
- rate_check: bfloat16 [3, 256, 8, 1024], P(None, 'gy', None, 'gz'), may hold values from -4 to 4
- levels_check: bfloat16 [2, 256, 8, 1024], P(None, 'gy', None, 'gz'), may hold values from 0.049804688 to 0.5
- efield_seed: float32 [3, 256, 8, 1024], P(None, 'gy', None, 'gz'), may hold values from -6 to 6
- hfield_seed: float32 [3, 256, 8, 1024], P(None, 'gy', None, 'gz'), may hold values from -6 to 6
- polar_seed: float32 [3, 256, 8, 1024], P(None, 'gy', None, 'gz'), may hold values from -6 to 6
- rate_seed: float32 [3, 256, 8, 1024], P(None, 'gy', None, 'gz'), may hold values from -6 to 6
- levels_seed: float32 [2, 256, 8, 1024], P(None, 'gy', None, 'gz'), may hold values from -6 to 6
- material_labels: int32 [256, 8, 1024], P('gy', None, 'gz'), may hold values from 0 to 3
- gain_labels: int32 [256, 8, 1024], P('gy', None, 'gz'), may hold values 0 or 1
- inverse_table: float32 [4], replicated, may hold values from 0.08 to 1
- source_field: float32 [256, 8, 1024], P('gy', None, 'gz'), may hold values from -6 to 6
- start_step: int32 [1], replicated, may hold values from 0 to 255
Outputs:
- efield_grad: float32 [3, 256, 8, 1024], P(None, 'gy', None, 'gz')
- hfield_grad: float32 [3, 256, 8, 1024], P(None, 'gy', None, 'gz')
- polar_grad: float32 [3, 256, 8, 1024], P(None, 'gy', None, 'gz')
- rate_grad: float32 [3, 256, 8, 1024], P(None, 'gy', None, 'gz')
- levels_grad: float32 [2, 256, 8, 1024], P(None, 'gy', None, 'gz')
- cell_grad: float32 [256, 8, 1024], P('gy', None, 'gz')
- table_grad: float32 [4], replicated
The draws below stay inside these ranges and needn't reach their ends.
All inputs are finite; a program needn't handle non-finite values. No bound on the sum of `gain_labels` on one device may be relied on, other than what follows from the above.
Results may differ from the reference program's by a relative error of at most 0.0003.
Values may be sent and summed in bfloat16 or wider, within the bound.
A program may use at most 64 MiB of HBM per device.

```python
import math
import jax
import jax.numpy as jnp
from jax import lax

SLAB = 8
MATERIALS = 4
NY = 256
NZ = 1024


def set_ends(values, rng, least, largest):
    longest = values.shape.index(max(values.shape))
    spots = []
    for shift in (0, 1):
        where = [jax.random.randint(jax.random.fold_in(rng, axis), (), 0, length) for axis, length in enumerate(values.shape)]
        where[longest] = (where[longest] + shift) % values.shape[longest]
        spots.append(tuple(where))
    return values.at[spots[0]].set(least).at[spots[1]].set(largest)


def level_of(own_key, dims, cuts, smallest, high):
    def one(dim, shards_of):
        heights = jax.random.uniform(jax.random.fold_in(jax.random.fold_in(own_key, 6), dim), (shards_of,), jnp.float32, smallest / len(cuts), high / len(cuts))
        return jnp.repeat(jnp.exp(heights), dims[dim] // shards_of).reshape((-1,) + (1,) * (len(dims) - dim - 1))

    factor_of = one(*cuts[0])
    for cut in cuts[1:]:
        factor_of = factor_of * one(*cut)
    return factor_of


def centred(stream_key, extent, scale, most, cuts=(), held_as=jnp.bfloat16):
    array = jax.random.normal(stream_key, extent, jnp.float32) * scale
    if len(cuts) > 0:
        array = level_of(stream_key, extent, cuts, -0.22, 0.18) * array
    return jnp.clip(array, min=-most, max=most).astype(held_as)


def setup_inputs(seed: int = 0) -> dict:
    keys = jax.random.split(jax.random.key(seed), 16)
    return {
        "efield_check": centred(keys[0], (3, NY, SLAB, NZ), 1.0, 6.0, ((1, 8), (3, 4))),
        "hfield_check": centred(keys[1], (3, NY, SLAB, NZ), 1.0, 6.0, ((1, 8), (3, 4))),
        "polar_check": centred(keys[2], (3, NY, SLAB, NZ), 0.5, 4.0, ((1, 8), (3, 4))),
        "rate_check": centred(keys[3], (3, NY, SLAB, NZ), 0.5, 4.0, ((1, 8), (3, 4))),
        "levels_check": jnp.clip(0.049804688 + 0.4501953 * jax.random.uniform(keys[4], (2, NY, SLAB, NZ), jnp.float32) ** level_of(keys[4], (2, NY, SLAB, NZ), ((1, 8), (3, 4)), -0.2, 0.2), 0.049804688, 0.5).astype(jnp.bfloat16),
        "efield_seed": centred(keys[5], (3, NY, SLAB, NZ), 1.0, 6.0, ((1, 8), (3, 4)), jnp.float32),
        "hfield_seed": centred(keys[6], (3, NY, SLAB, NZ), 1.0, 6.0, ((1, 8), (3, 4)), jnp.float32),
        "polar_seed": centred(keys[7], (3, NY, SLAB, NZ), 1.0, 6.0, ((1, 8), (3, 4)), jnp.float32),
        "rate_seed": centred(keys[8], (3, NY, SLAB, NZ), 1.0, 6.0, ((1, 8), (3, 4)), jnp.float32),
        "levels_seed": centred(keys[9], (2, NY, SLAB, NZ), 1.0, 6.0, ((1, 8), (3, 4)), jnp.float32),
        "material_labels": set_ends(jax.random.randint(keys[10], (NY, SLAB, NZ), 0, MATERIALS), jax.random.fold_in(keys[10], 1), 0, MATERIALS - 1).astype(jnp.int32),
        "gain_labels": set_ends((jax.random.randint(keys[11], (NY, SLAB, NZ), 0, 2) < 1).astype(jnp.int32), jax.random.fold_in(keys[11], 1), 0, 1),
        "inverse_table": jnp.clip(jnp.exp(jax.random.uniform(keys[12], (MATERIALS,), jnp.float32, math.log(0.08), math.log(1.0))), 0.08, 1.0),
        "source_field": centred(keys[13], (NY, SLAB, NZ), 1.0, 6.0, ((0, 8), (2, 4)), jnp.float32),
        "start_step": jax.random.randint(keys[14], (1,), 0, 256).astype(jnp.int32),
    }


MAGNETIC_STEP = 0.5
ELECTRIC_STEP = 0.5
TIME_STEP = 0.5
DAMPING = 0.9
STIFFNESS = 0.3
COUPLING = 0.4
PUMPING = 0.05
UPPER_DECAY = 0.02
LOWER_DECAY = 0.3
STIMULATED = 0.2
SOURCE_OMEGA = 0.35

def front(values, axis):
    rest = lax.slice_in_dim(values, 1, values.shape[axis], axis=axis)
    border = jnp.zeros_like(lax.slice_in_dim(values, 0, 1, axis=axis))
    return jnp.concatenate([rest, border], axis)

def behind(values, axis):
    rest = lax.slice_in_dim(values, 0, values.shape[axis] - 1, axis=axis)
    border = jnp.zeros_like(lax.slice_in_dim(values, 0, 1, axis=axis))
    return jnp.concatenate([border, rest], axis)

def curl_from(along_x, along_y, along_z):
    return jnp.stack([along_y[2] - along_z[1], along_z[0] - along_x[2], along_x[1] - along_y[0]])

def curl_forward(field):
    return curl_from(front(field, 2) - field, front(field, 1) - field, front(field, 3) - field)

def curl_backward(field):
    return curl_from(field - behind(field, 2), field - behind(field, 1), field - behind(field, 3))

def local_update(efield, polar_field, polar_rate, levels, curl_field, inverse, gain_region, source_push):
    rate_next = DAMPING * polar_rate - STIFFNESS * polar_field + COUPLING * gain_region * (levels[0] - levels[1]) * efield
    polar_next = polar_field + TIME_STEP * rate_next
    forcing = ELECTRIC_STEP * curl_field - (polar_next - polar_field)
    forcing = jnp.concatenate([forcing[:2], forcing[2:] - source_push[None]], 0)
    efield_next = efield + inverse * forcing
    stimulated = STIMULATED * gain_region * lax.optimization_barrier(jnp.sum(efield_next * rate_next, axis=0))
    upper = levels[0] + TIME_STEP * (PUMPING * (1.0 - levels[0] - levels[1]) - UPPER_DECAY * levels[0]) - stimulated
    lower = levels[1] + TIME_STEP * (UPPER_DECAY * levels[0] - LOWER_DECAY * levels[1]) + stimulated
    return (efield_next, polar_next, rate_next, jnp.stack([upper, lower]))

def reverse_local(efield, polar_field, polar_rate, levels, curl_field, inverse, gain_region, source_push, seeds):

    def update(first, second, third, fourth, fifth, sixth):
        return local_update(first, second, third, fourth, fifth, sixth, gain_region, source_push)
    unused, pullback = jax.vjp(update, efield, polar_field, polar_rate, levels, curl_field, inverse)
    return pullback(seeds)

def material_map(material_labels, inverse_table):
    inverse = jnp.zeros(material_labels.shape, jnp.float32)
    for label in range(inverse_table.shape[0]):
        inverse = inverse + jnp.where(material_labels == label, inverse_table[label], jnp.float32(0.0))
    return inverse

def label_sums(material_labels, values, count):
    return jnp.stack([jnp.sum(jnp.where(material_labels == label, values, jnp.float32(0.0))) for label in range(count)])

def reference(efield_check, hfield_check, polar_check, rate_check, levels_check, efield_seed, hfield_seed, polar_seed, rate_seed, levels_seed, material_labels, gain_labels, inverse_table, source_field, start_step):
    inverse = material_map(material_labels, inverse_table)
    gain_region = gain_labels.astype(jnp.float32)
    start = start_step[0].astype(jnp.float32)
    push_first = jnp.sin(SOURCE_OMEGA * start) * source_field
    push_second = jnp.sin(SOURCE_OMEGA * (start + 1.0)) * source_field
    efield = efield_check.astype(jnp.float32)
    hfield = hfield_check.astype(jnp.float32)
    polar_field = polar_check.astype(jnp.float32)
    polar_rate = rate_check.astype(jnp.float32)
    levels = levels_check.astype(jnp.float32)
    hfield_mid = hfield - MAGNETIC_STEP * curl_forward(efield)
    curl_first = curl_backward(hfield_mid)
    state_one = local_update(efield, polar_field, polar_rate, levels, curl_first, inverse, gain_region, push_first)
    hfield_next = hfield_mid - MAGNETIC_STEP * curl_forward(state_one[0])
    curl_second = curl_backward(hfield_next)
    back_e, back_p, back_q, back_n, back_c, grad_second = reverse_local(state_one[0], state_one[1], state_one[2], state_one[3], curl_second, inverse, gain_region, push_second, (efield_seed, polar_seed, rate_seed, levels_seed))
    h_back = hfield_seed + curl_forward(back_c)
    e_back = back_e - MAGNETIC_STEP * curl_backward(h_back)
    last_e, polar_grad, rate_grad, levels_grad, last_c, grad_first = reverse_local(efield, polar_field, polar_rate, levels, curl_first, inverse, gain_region, push_first, (e_back, back_p, back_q, back_n))
    hfield_grad = h_back + curl_forward(last_c)
    efield_grad = last_e - MAGNETIC_STEP * curl_backward(hfield_grad)
    cell_grad = grad_second + grad_first
    table_grad = label_sums(material_labels, cell_grad, inverse_table.shape[0]) * (1.0 / math.sqrt(NY * SLAB * NZ))
    return (efield_grad, hfield_grad, polar_grad, rate_grad, levels_grad, cell_grad, table_grad)
```

```python
import functools
import math

import jax
import jax.numpy as jnp
from jax import lax
from jax.experimental import pallas as pl
from jax.experimental.pallas import tpu as pltpu
from jax.sharding import PartitionSpec as P

MAGNETIC_STEP = 0.5
ELECTRIC_STEP = 0.5
TIME_STEP = 0.5
DAMPING = 0.9
STIFFNESS = 0.3
COUPLING = 0.4
PUMPING = 0.05
UPPER_DECAY = 0.02
LOWER_DECAY = 0.3
STIMULATED = 0.2
SOURCE_OMEGA = 0.35

MESH = pl.DeviceIdType.MESH
LANES = 128
FIELDS = (1, 2, 1)
BASES = (2, 2, 0)
UP = tuple(3 * f + b for f, b in zip(FIELDS, BASES))
DOWN = tuple(2 * f for f in FIELDS)
UP_AT = tuple(sum(UP[:k]) for k in range(3))
DOWN_AT = tuple(sum(DOWN[:k]) for k in range(3))
DIAG_AT = tuple(sum(FIELDS[:k]) for k in range(3))


def kernel(
    ngy,
    ngz,
    count,
    scale,
    e_in, h_in, p_in, q_in, n_in,
    es_in, hs_in, ps_in, qs_in, ns_in,
    lab_in, gain_in, table, src_in, start,
    eg_out, hg_out, pg_out, qg_out, ng_out, cg_out, tg_out,
    e_v, h_v, p_v, q_v, n_v,
    es_v, hs_v, ps_v, qs_v, ns_v,
    lab_v, gain_v, src_v,
    ef, m, e1, ac, q1, q2, f1, k1, cc, hg, eg, pg, qg, ng, cg,
    m_col, b_col,
    yu_s, yu_r, yd_s, yd_r, zu_s, zu_r, zd_s, zd_r, a_r, b_r,
    sums, part_z, part_y,
    in_sem, out_sem, send_sem, recv_sem,
    zs_sem, zr_sem, ys_sem, yr_sem,
):
    gy = lax.axis_index("gy")
    gz = lax.axis_index("gz")
    rows, depth, width = e_v.shape[1], e_v.shape[2], e_v.shape[3]

    pairs = (
        (e_in, e_v), (h_in, h_v), (q_in, q_v), (p_in, p_v), (n_in, n_v),
        (lab_in, lab_v), (gain_in, gain_v), (src_in, src_v), (es_in, es_v),
        (ns_in, ns_v), (hs_in, hs_v), (qs_in, qs_v), (ps_in, ps_v),
    )
    loads = [
        pltpu.make_async_copy(a, b, in_sem.at[i]) for i, (a, b) in enumerate(pairs)
    ]
    for copy in loads:
        copy.start()

    for ref in (yu_r, yd_r, zu_r, zd_r, a_r, b_r, zu_s, zd_s):
        ref[...] = jnp.zeros(ref.shape, ref.dtype)

    has_down, has_up = gy > 0, gy < ngy - 1
    has_left, has_right = gz > 0, gz < ngz - 1
    diag_a = jnp.logical_and(has_up, has_left)
    diag_b = jnp.logical_and(has_down, has_right)

    barrier = pltpu.get_barrier_semaphore()

    def greet_y(d, _):
        pl.semaphore_signal(
            barrier, inc=1, device_id=(lax.rem(gy + d, ngy), gz), device_id_type=MESH
        )
        return _

    def greet_z(d, _):
        pl.semaphore_signal(
            barrier, inc=1, device_id=(gy, lax.rem(gz + d, ngz)), device_id_type=MESH
        )
        return _

    lax.fori_loop(1, ngy, greet_y, 0)
    lax.fori_loop(1, ngz, greet_z, 0)

    @pl.when(diag_a)
    def _():
        pl.semaphore_signal(barrier, inc=1, device_id=(gy + 1, gz - 1), device_id_type=MESH)

    @pl.when(diag_b)
    def _():
        pl.semaphore_signal(barrier, inc=1, device_id=(gy - 1, gz + 1), device_id_type=MESH)

    def links(k):
        f = FIELDS[k]
        up = pl.ds(UP_AT[k], UP[k])
        down = pl.ds(DOWN_AT[k], DOWN[k])
        diag = pl.ds(DIAG_AT[k], f)
        return (
            (yu_s.at[up], yu_r.at[up], (gy + 1, gz), has_up, has_down),
            (yd_s.at[down], yd_r.at[down], (gy - 1, gz), has_down, has_up),
            (zu_s.at[up], zu_r.at[up], (gy, gz + 1), has_right, has_left),
            (zd_s.at[down], zd_r.at[down], (gy, gz - 1), has_left, has_right),
            (zd_s.at[pl.ds(DOWN_AT[k] + f, f)], a_r.at[diag], (gy + 1, gz - 1), diag_a, diag_b),
            (zu_s.at[pl.ds(UP_AT[k] + 2 * f, f)], b_r.at[diag], (gy - 1, gz + 1), diag_b, diag_a),
        )

    def remote(k, i, link):
        return pltpu.make_async_remote_copy(
            src_ref=link[0],
            dst_ref=link[1],
            send_sem=send_sem.at[k, i],
            recv_sem=recv_sem.at[k, i],
            device_id=link[2],
            device_id_type=MESH,
        )

    def send(k):
        for i, link in enumerate(links(k)):

            @pl.when(link[3])
            def _(i=i, link=link):
                remote(k, i, link).start()

    def receive(k):
        for i, link in enumerate(links(k)):

            @pl.when(link[4])
            def _(i=i, link=link):
                remote(k, i, link).wait_recv()

    def finish(k):
        for i, link in enumerate(links(k)):

            @pl.when(link[3])
            def _(i=i, link=link):
                remote(k, i, link).wait_send()

    lane_wide = lax.broadcasted_iota(jnp.int32, (depth, width), 1)
    sub_wide = lax.broadcasted_iota(jnp.int32, (depth, width), 0)
    lane = lax.broadcasted_iota(jnp.int32, (depth, LANES), 1)
    sub = lax.broadcasted_iota(jnp.int32, (depth, LANES), 0)
    last_lane = lane_wide == width - 1
    first_lane = lane_wide == 0
    tiles = width // LANES

    def widen(tile):
        return tile if tiles == 1 else jnp.concatenate([tile] * tiles, axis=1)

    def x_front(v):
        s = sub_wide if v.shape[1] == width else sub
        return jnp.where(s == depth - 1, 0.0, pltpu.roll(v, depth - 1, 0))

    def x_behind(v):
        return jnp.where(sub_wide == 0, 0.0, pltpu.roll(v, 1, 0))

    def z_front(v, tile, r):
        border = pltpu.roll(tile, LANES - 1 - r, 1)
        return jnp.where(last_lane, widen(border), pltpu.roll(v, width - 1, 1))

    def z_behind(v, tile, r):
        border = pltpu.roll(tile, lax.rem(LANES - r, LANES), 1)
        return jnp.where(first_lane, widen(border), pltpu.roll(v, 1, 1))

    def curl_forward(ref, k, j, r):
        f = FIELDS[k]
        vx, vy, vz = ref[0, r], ref[1, r], ref[2, r]
        dy_x, dy_z = ref[0, r + 1] - vx, ref[2, r + 1] - vz
        dz_x = z_front(vx, zd_r[DOWN_AT[k] + j], r) - vx
        dz_y = z_front(vy, zd_r[DOWN_AT[k] + f + j], r) - vy
        dx_y, dx_z = x_front(vy) - vy, x_front(vz) - vz
        return (dy_z - dz_y, dz_x - dx_z, dx_y - dy_x)

    def curl_backward(vx, vy, vz, back_x, back_z, col, r):
        dy_x, dy_z = vx - back_x, vz - back_z
        dz_x = vx - z_behind(vx, col[0], r)
        dz_y = vy - z_behind(vy, col[1], r)
        dx_y, dx_z = vy - x_behind(vy), vz - x_behind(vz)
        return (dy_z - dz_y, dz_x - dx_z, dx_y - dy_x)

    def border_row(ref, k, j):
        f = FIELDS[k]
        vx, vy, vz = (yu_r[UP_AT[k] + c * f + j] for c in range(3))
        dz_y = z_front(vy, a_r[DIAG_AT[k] + j], rows - 1) - vy
        dy_x, dy_z = ref[0, 0] - vx, ref[2, 0] - vz
        return dy_z - dz_y, x_front(vy) - vy - dy_x

    def border_col(k, j):
        f = FIELDS[k]
        vx, vy, vz = (zu_r[UP_AT[k] + c * f + j] for c in range(3))
        corner = pltpu.roll(b_r[DIAG_AT[k] + j], rows - 1, 1)
        dy_z = jnp.where(lane == rows - 1, corner, pltpu.roll(vz, LANES - 1, 1)) - vz
        dz_x = zd_s[DOWN_AT[k] + j] - vx
        dz_y = zd_s[DOWN_AT[k] + f + j] - vy
        return dy_z - dz_y, dz_x - (x_front(vz) - vz)

    row_on = jnp.where(has_down, 1.0, 0.0).astype(jnp.float32)
    col_on = jnp.where(has_left, 1.0, 0.0).astype(jnp.float32)

    def pack(ref, slot, r, column):
        ref[slot] = jnp.where(lane == r, jnp.broadcast_to(column, (depth, LANES)), ref[slot])

    def pack_first(k, j, r, vx, vy):
        f = FIELDS[k]
        pack(zd_s, DOWN_AT[k] + j, r, vx[:, :1])
        pack(zd_s, DOWN_AT[k] + f + j, r, vy[:, :1])

    def pack_last(k, j, r, values):
        f = FIELDS[k]
        for c, v in enumerate(values):
            pack(zu_s, UP_AT[k] + c * f + j, r, v[:, width - 1 :])

    def pack_base(k, r, vx, vy):
        pack(zu_s, UP_AT[k] + 3 * FIELDS[k], r, vx[:, width - 1 :])
        pack(zu_s, UP_AT[k] + 3 * FIELDS[k] + 1, r, vy[:, width - 1 :])

    def stage_rows(k, j, ref):
        f = FIELDS[k]
        for c in range(3):
            yu_s[UP_AT[k] + c * f + j] = ref[c, rows - 1]
        yd_s[DOWN_AT[k] + j] = ref[0, 0]
        yd_s[DOWN_AT[k] + f + j] = ref[2, 0]

    def take_rows(k, j, ref):
        f = FIELDS[k]
        ref[0, rows] = yd_r[DOWN_AT[k] + j]
        ref[2, rows] = yd_r[DOWN_AT[k] + f + j]

    loads[0].wait()
    loads[1].wait()

    def first_pass(r, _):
        v = [e_v[c, r].astype(jnp.float32) for c in range(3)]
        for c in range(3):
            ef[c, r] = v[c]
        pack_first(0, 0, r, v[0], v[1])
        pack_last(0, 0, r, v)
        pack_base(0, r, h_v[0, r].astype(jnp.float32), h_v[1, r].astype(jnp.float32))
        return _

    lax.fori_loop(0, rows, first_pass, 0)
    stage_rows(0, 0, ef)
    yu_s[UP_AT[0] + 3] = h_v[0, rows - 1].astype(jnp.float32)
    yu_s[UP_AT[0] + 4] = h_v[2, rows - 1].astype(jnp.float32)

    greeted = (
        (ngy - 1) + (ngz - 1) + jnp.where(diag_a, 1, 0) + jnp.where(diag_b, 1, 0)
    )
    pl.semaphore_wait(barrier, greeted)
    send(0)

    begin = start[0].astype(jnp.float32)
    sine_first = jnp.sin(jnp.full((depth, LANES), SOURCE_OMEGA * begin, jnp.float32))
    sine_second = jnp.sin(jnp.full((depth, LANES), SOURCE_OMEGA * (begin + 1.0), jnp.float32))
    sine_first, sine_second = widen(sine_first), widen(sine_second)

    for copy in loads[2:11]:
        copy.wait()

    def inverse_of(labels):
        value = jnp.full(labels.shape, table[0], jnp.float32)
        for label in range(1, count):
            value = jnp.where(labels == label, table[label], value)
        return value

    receive(0)
    take_rows(0, 0, ef)
    row_x, row_z = border_row(ef, 0, 0)
    m[0, 0] = row_on * (yu_r[UP_AT[0] + 3] - MAGNETIC_STEP * row_x)
    m[2, 0] = row_on * (yu_r[UP_AT[0] + 4] - MAGNETIC_STEP * row_z)
    col_x, col_y = border_col(0, 0)
    m_col[0] = col_on * (zu_r[UP_AT[0] + 3] - MAGNETIC_STEP * col_x)
    m_col[1] = col_on * (zu_r[UP_AT[0] + 4] - MAGNETIC_STEP * col_y)

    def forward_pass(r, _):
        curl = curl_forward(ef, 0, 0, r)
        mid = [h_v[c, r].astype(jnp.float32) - MAGNETIC_STEP * curl[c] for c in range(3)]
        for c in range(3):
            m[c, r + 1] = mid[c]
        c1 = curl_backward(*mid, m[0, r], m[2, r], m_col, r)
        inverse = inverse_of(lab_v[r])
        gain = gain_v[r].astype(jnp.float32)
        source = src_v[r]
        upper, lower = n_v[0, r].astype(jnp.float32), n_v[1, r].astype(jnp.float32)
        gain_c, gain_s = COUPLING * gain, STIMULATED * gain
        couple = gain_c * (upper - lower)
        nexts, rates, polars = [], [], []
        work = None
        for c in range(3):
            e, p, q = ef[c, r], p_v[c, r].astype(jnp.float32), q_v[c, r].astype(jnp.float32)
            rate = DAMPING * q - STIFFNESS * p + couple * e
            polars.append(p + TIME_STEP * rate)
            force = ELECTRIC_STEP * c1[c] - TIME_STEP * rate
            if c == 2:
                force = force - sine_first * source
            new = e + inverse * force
            q1[c, r] = rate
            f1[c, r] = force
            e1[c, r] = new
            work = new * rate if work is None else work + new * rate
            nexts.append(new)
            rates.append(rate)
        s = gain_s * work
        upper_1 = upper + TIME_STEP * (PUMPING * (1.0 - upper - lower) - UPPER_DECAY * upper) - s
        lower_1 = lower + TIME_STEP * (UPPER_DECAY * upper - LOWER_DECAY * lower) + s
        couple_1 = gain_c * (upper_1 - lower_1)
        k1[r] = couple_1
        t2 = gain_s * (ns_v[1, r] - ns_v[0, r])
        half = ELECTRIC_STEP * inverse
        adj = []
        for c in range(3):
            rate = DAMPING * rates[c] - STIFFNESS * polars[c] + couple_1 * nexts[c]
            q2[c, r] = rate
            adj.append(half * (es_v[c, r] + t2 * rate))
            ac[c, r] = adj[c]
        pack_first(1, 0, r, nexts[0], nexts[1])
        pack_last(1, 0, r, nexts)
        pack_first(1, 1, r, adj[0], adj[1])
        pack_last(1, 1, r, adj)
        pack_base(1, r, hs_v[0, r], hs_v[1, r])
        return _

    lax.fori_loop(0, rows, forward_pass, 0)

    stage_rows(1, 0, e1)
    stage_rows(1, 1, ac)
    yu_s[UP_AT[1] + 6] = hs_v[0, rows - 1]
    yu_s[UP_AT[1] + 7] = hs_v[2, rows - 1]
    send(1)
    for copy in loads[11:]:
        copy.wait()
    receive(1)
    take_rows(1, 0, e1)
    take_rows(1, 1, ac)
    row_x, row_z = border_row(e1, 1, 0)
    m[0, 0] = m[0, 0] - MAGNETIC_STEP * (row_on * row_x)
    m[2, 0] = m[2, 0] - MAGNETIC_STEP * (row_on * row_z)
    row_x, row_z = border_row(ac, 1, 1)
    hg[0, 0] = row_on * (yu_r[UP_AT[1] + 6] + row_x)
    hg[2, 0] = row_on * (yu_r[UP_AT[1] + 7] + row_z)
    col_x, col_y = border_col(1, 0)
    m_col[0] = m_col[0] - MAGNETIC_STEP * (col_on * col_x)
    m_col[1] = m_col[1] - MAGNETIC_STEP * (col_on * col_y)
    col_x, col_y = border_col(1, 1)
    b_col[0] = col_on * (zu_r[UP_AT[1] + 6] + col_x)
    b_col[1] = col_on * (zu_r[UP_AT[1] + 7] + col_y)
    sums[...] = jnp.zeros(sums.shape, jnp.float32)

    keep_upper = 1.0 - TIME_STEP * (PUMPING + UPPER_DECAY)
    feed_upper = TIME_STEP * UPPER_DECAY
    drain_lower = -TIME_STEP * PUMPING
    keep_lower = 1.0 - TIME_STEP * LOWER_DECAY

    def backward_pass(r, _):
        curl = curl_forward(e1, 1, 0, r)
        last = [m[c, r + 1] - MAGNETIC_STEP * curl[c] for c in range(3)]
        back_x, back_z = m[0, r], m[2, r]
        m[0, r + 1] = last[0]
        m[2, r + 1] = last[2]
        c2 = curl_backward(*last, back_x, back_z, m_col, r)
        curl = curl_forward(ac, 1, 1, r)
        hb = [hs_v[c, r] + curl[c] for c in range(3)]
        for c in range(3):
            hg[c, r + 1] = hb[c]
        eb = curl_backward(*hb, hg[0, r], hg[2, r], b_col, r)

        labels = lab_v[r]
        inverse = inverse_of(labels)
        gain = gain_v[r].astype(jnp.float32)
        source = src_v[r]
        gain_c, gain_s = COUPLING * gain, STIMULATED * gain
        seed_u, seed_l = ns_v[0, r], ns_v[1, r]
        t2 = gain_s * (seed_l - seed_u)
        couple_1 = k1[r]
        total = None
        overlap = None
        b_e, a_p, a_q = [], [], []
        for c in range(3):
            e, rate = e1[c, r], q2[c, r]
            force = ELECTRIC_STEP * c2[c] - TIME_STEP * rate
            if c == 2:
                force = force - sine_second * source
            new = e + inverse * force
            adj_e = es_v[c, r] + t2 * rate
            term = adj_e * force
            total = term if total is None else total + term
            seed_p = ps_v[c, r]
            adj_q = qs_v[c, r] + t2 * new + TIME_STEP * (seed_p - inverse * adj_e)
            a_p.append(seed_p - STIFFNESS * adj_q)
            a_q.append(DAMPING * adj_q)
            b_e.append(adj_e + couple_1 * adj_q - MAGNETIC_STEP * eb[c])
            overlap = adj_q * e if overlap is None else overlap + adj_q * e
        bend = gain_c * overlap
        a_u = keep_upper * seed_u + feed_upper * seed_l + bend
        a_l = drain_lower * seed_u + keep_lower * seed_l - bend

        t1 = gain_s * (a_l - a_u)
        upper, lower = n_v[0, r].astype(jnp.float32), n_v[1, r].astype(jnp.float32)
        couple = gain_c * (upper - lower)
        overlap = None
        out = []
        for c in range(3):
            rate = q1[c, r]
            adj_e = b_e[c] + t1 * rate
            total = total + adj_e * f1[c, r]
            adj_f = inverse * adj_e
            curl_adj = ELECTRIC_STEP * adj_f
            out.append(curl_adj)
            cc[c, r] = curl_adj
            adj_q = a_q[c] + t1 * e1[c, r] + TIME_STEP * (a_p[c] - adj_f)
            pg[c, r] = a_p[c] - STIFFNESS * adj_q
            qg[c, r] = DAMPING * adj_q
            eg[c, r] = adj_e + couple * adj_q
            e = ef[c, r]
            overlap = adj_q * e if overlap is None else overlap + adj_q * e
        bend = gain_c * overlap
        ng[0, r] = keep_upper * a_u + feed_upper * a_l + bend
        ng[1, r] = drain_lower * a_u + keep_lower * a_l - bend
        cg[r] = total
        for label in range(count):
            sums[label] = sums[label] + jnp.where(labels == label, total, 0.0)
        pack_first(2, 0, r, out[0], out[1])
        pack_last(2, 0, r, out)
        return _

    lax.fori_loop(0, rows, backward_pass, 0)

    stage_rows(2, 0, cc)
    send(2)

    stores = [
        pltpu.make_async_copy(a, b, out_sem.at[i])
        for i, (a, b) in enumerate(
            (
                (pg, pg_out), (qg, qg_out), (ng, ng_out), (cg, cg_out),
                (hg.at[:, pl.ds(1, rows)], hg_out), (eg, eg_out),
            )
        )
    ]
    for copy in stores[:4]:
        copy.start()

    mine = jnp.zeros(part_z.shape[1:], jnp.float32)
    part_sub = lax.broadcasted_iota(jnp.int32, mine.shape, 0)
    for label in range(count):
        narrow = sum(sums[label, :, t * LANES : (t + 1) * LANES] for t in range(tiles))
        mine = jnp.where(part_sub == label, jnp.sum(narrow, axis=0, keepdims=True), mine)
    part_z[gz] = mine

    def gather(part, n, me, device, s_sem, r_sem):
        def copy_to(d):
            return pltpu.make_async_remote_copy(
                src_ref=part.at[me],
                dst_ref=part.at[me],
                send_sem=s_sem.at[d],
                recv_sem=r_sem.at[me],
                device_id=device(lax.rem(me + d, n)),
                device_id_type=MESH,
            )

        def copy_from(d):
            other = lax.rem(me + d, n)
            return pltpu.make_async_remote_copy(
                src_ref=part.at[other],
                dst_ref=part.at[other],
                send_sem=s_sem.at[d],
                recv_sem=r_sem.at[other],
                device_id=device(other),
                device_id_type=MESH,
            )

        def each(act):
            def body(d, _):
                act(d)
                return _

            lax.fori_loop(1, n, body, 0)

        return (
            lambda: each(lambda d: copy_to(d).start()),
            lambda: each(lambda d: copy_from(d).wait_recv()),
            lambda: each(lambda d: copy_to(d).wait_send()),
        )

    z_start, z_wait, z_sent = gather(part_z, ngz, gz, lambda o: (gy, o), zs_sem, zr_sem)
    y_start, y_wait, y_sent = gather(part_y, ngy, gy, lambda o: (o, gz), ys_sem, yr_sem)
    z_start()

    receive(2)
    take_rows(2, 0, cc)
    row_x, row_z = border_row(cc, 2, 0)
    hg[0, 0] = hg[0, 0] + row_on * row_x
    hg[2, 0] = hg[2, 0] + row_on * row_z
    col_x, col_y = border_col(2, 0)
    b_col[0] = b_col[0] + col_on * col_x
    b_col[1] = b_col[1] + col_on * col_y

    z_wait()
    part_y[gy] = jnp.sum(part_z[...], axis=0)
    y_start()

    def last_pass(r, _):
        curl = curl_forward(cc, 2, 0, r)
        out = [hg[c, r + 1] + curl[c] for c in range(3)]
        for c in range(3):
            hg[c, r + 1] = out[c]
        back = curl_backward(*out, hg[0, r], hg[2, r], b_col, r)
        for c in range(3):
            eg[c, r] = eg[c, r] - MAGNETIC_STEP * back[c]
        return _

    lax.fori_loop(0, rows, last_pass, 0)
    for copy in stores[4:]:
        copy.start()

    y_wait()
    whole = jnp.sum(part_y[...], axis=0)
    for label in range(count):
        tg_out[label] = jnp.sum(whole[label : label + 1, :]) * scale

    for k in range(3):
        finish(k)
    z_sent()
    y_sent()
    for copy in stores:
        copy.wait()


def solution(mesh):
    ngy, ngz = mesh.shape["gy"], mesh.shape["gz"]

    def on_device(*arrays):
        shape = arrays[0].shape
        _, rows, depth, width = shape
        count = arrays[12].shape[0]
        cells = rows * depth * width * ngy * ngz
        f32 = jnp.float32
        space = pl.BlockSpec(memory_space=pl.ANY)
        scalar = pl.BlockSpec(memory_space=pltpu.SMEM)
        three = jax.ShapeDtypeStruct(shape, f32)
        two = jax.ShapeDtypeStruct((2,) + shape[1:], f32)
        one = jax.ShapeDtypeStruct(shape[1:], f32)

        def vm(lead, wide=width):
            return pltpu.VMEM((lead, depth, wide), f32)

        def field(n, extra=0):
            return pltpu.VMEM((n, rows + extra, depth, width), f32)

        inputs = [
            pltpu.VMEM(arrays[i].shape, arrays[i].dtype) for i in (0, 1, 2, 3, 4, 5, 6, 7, 8, 9, 10, 11, 13)
        ]
        slots = -(-count // 8) * 8
        up, down, diag = sum(UP), sum(DOWN), sum(FIELDS)
        dma = pltpu.SemaphoreType.DMA
        scratch = inputs + [
            field(3, 1), field(3, 1), field(3, 1), field(3, 1),
            field(3), field(3), field(3), pltpu.VMEM(shape[1:], f32),
            field(3, 1), field(3, 1), field(3), field(3), field(3), field(2),
            pltpu.VMEM(shape[1:], f32),
            vm(2, LANES), vm(2, LANES),
            vm(up), vm(up), vm(down), vm(down),
            vm(up, LANES), vm(up, LANES), vm(down, LANES), vm(down, LANES),
            vm(diag, LANES), vm(diag, LANES),
            vm(count),
            pltpu.VMEM((ngz, slots, LANES), f32),
            pltpu.VMEM((ngy, slots, LANES), f32),
            dma((13,)), dma((6,)), dma((3, 6)), dma((3, 6)),
            dma((ngz,)), dma((ngz,)), dma((ngy,)), dma((ngy,)),
        ]
        moved = 4 * rows * depth * width * 40
        return pl.pallas_call(
            functools.partial(kernel, ngy, ngz, count, 1.0 / math.sqrt(cells)),
            out_shape=(three, three, three, three, two, one, jax.ShapeDtypeStruct((count,), f32)),
            in_specs=[scalar if i in (12, 14) else space for i in range(15)],
            out_specs=(space,) * 6 + (scalar,),
            scratch_shapes=scratch,
            cost_estimate=pl.CostEstimate(
                flops=500 * rows * depth * width, bytes_accessed=moved, transcendentals=0
            ),
            compiler_params=pltpu.CompilerParams(
                collective_id=0, has_side_effects=True, vmem_limit_bytes=56 * 1024 * 1024
            ),
        )(*arrays)

    field = P(None, "gy", None, "gz")
    cell = P("gy", None, "gz")
    return jax.shard_map(
        on_device,
        mesh=mesh,
        in_specs=(field,) * 10 + (cell, cell, P(), cell, P()),
        out_specs=(field,) * 5 + (cell, P()),
        check_vma=False,
    )
```

```python
import functools
import math

import jax
import jax.numpy as jnp
from jax import lax
from jax.experimental import pallas as pl
from jax.experimental.pallas import tpu as pltpu
from jax.sharding import PartitionSpec as P

MAGNETIC_STEP = 0.5
ELECTRIC_STEP = 0.5
TIME_STEP = 0.5
DAMPING = 0.9
STIFFNESS = 0.3
COUPLING = 0.4
PUMPING = 0.05
UPPER_DECAY = 0.02
LOWER_DECAY = 0.3
STIMULATED = 0.2
SOURCE_OMEGA = 0.35

MESH = pl.DeviceIdType.MESH
LANES = 128
ROWS_PER_STEP = 4
FIELDS = (1, 2, 1)
BASES = (2, 2, 0)
UP = tuple(3 * f + b for f, b in zip(FIELDS, BASES))
DOWN = tuple(2 * f for f in FIELDS)
UP_AT = tuple(sum(UP[:k]) for k in range(3))
DOWN_AT = tuple(sum(DOWN[:k]) for k in range(3))
DIAG_AT = tuple(sum(FIELDS[:k]) for k in range(3))


class Shifts:
    def __init__(self, depth, width):
        self.depth, self.width, self.tiles = depth, width, width // LANES
        self.lane = lax.broadcasted_iota(jnp.int32, (depth, LANES), 1)

    def rows_of(self, v):
        return [v[u : u + self.depth] for u in range(0, v.shape[0], self.depth)]

    def widen(self, tile):
        return tile if self.tiles == 1 else jnp.concatenate([tile] * self.tiles, axis=1)

    def x_roll(self, v, shift, edge):
        s = lax.broadcasted_iota(jnp.int32, (self.depth, v.shape[1]), 0)
        rolled = [jnp.where(s == edge, 0.0, pltpu.roll(u, shift, 0)) for u in self.rows_of(v)]
        return jnp.concatenate(rolled, axis=0)

    def x_front(self, v):
        return self.x_roll(v, self.depth - 1, self.depth - 1)

    def x_behind(self, v):
        return self.x_roll(v, 1, 0)

    def z_front(self, v, tile, r):
        lanes = self.lane
        out = []
        for u, row in enumerate(self.rows_of(v)):
            border = pltpu.roll(tile, LANES - 1 - (r + u), 1)
            rolled = pltpu.roll(row, self.width - 1, 1)
            last = jnp.where(lanes == LANES - 1, border, rolled[:, self.width - LANES :])
            if self.tiles > 1:
                last = jnp.concatenate([rolled[:, : self.width - LANES], last], axis=1)
            out.append(last)
        return jnp.concatenate(out, axis=0)

    def z_behind(self, v, tile, r):
        lanes = self.lane
        out = []
        for u, row in enumerate(self.rows_of(v)):
            border = pltpu.roll(tile, lax.rem(LANES - (r + u), LANES), 1)
            rolled = pltpu.roll(row, 1, 1)
            first = jnp.where(lanes == 0, border, rolled[:, :LANES])
            if self.tiles > 1:
                first = jnp.concatenate([first, rolled[:, LANES:]], axis=1)
            out.append(first)
        return jnp.concatenate(out, axis=0)

    def curl_forward(self, ref, tile_x, tile_y, r, group):
        def load(c, at):
            return ref[c, pl.ds(at, group)].reshape(group * self.depth, self.width)

        vx, vy, vz = load(0, r), load(1, r), load(2, r)
        dy_x, dy_z = load(0, r + 1) - vx, load(2, r + 1) - vz
        dz_x = self.z_front(vx, tile_x, r) - vx
        dz_y = self.z_front(vy, tile_y, r) - vy
        dx_y, dx_z = self.x_front(vy) - vy, self.x_front(vz) - vz
        return (dy_z - dz_y, dz_x - dx_z, dx_y - dy_x)

    def curl_backward(self, v, back_x, back_z, col, r):
        vx, vy, vz = v

        def behind(row, whole):
            if whole.shape[0] == self.depth:
                return row
            return jnp.concatenate([row, whole[: -self.depth]], axis=0)

        dy_x, dy_z = vx - behind(back_x, vx), vz - behind(back_z, vz)
        dz_x = vx - self.z_behind(vx, col[0], r)
        dz_y = vy - self.z_behind(vy, col[1], r)
        dx_y, dx_z = vy - self.x_behind(vy), vz - self.x_behind(vz)
        return (dy_z - dz_y, dz_x - dx_z, dx_y - dy_x)


def kernel(
    ngy,
    ngz,
    count,
    scale,
    e_in, h_in, p_in, q_in, n_in,
    es_in, hs_in, ps_in, qs_in, ns_in,
    lab_in, gain_in, table, src_in, start,
    cc, hg, eg, pg, qg, ng, cg, tiles_out, b_col, tg_out,
    e_v, h_v, p_v, q_v, n_v,
    es_v, hs_v, ps_v, qs_v, ns_v,
    lab_v, gain_v, src_v,
    ef, m, e1, ac, q1, q2, f1, k1,
    m_col,
    yu_s, yu_r, yd_s, yd_r, zu_s, zu_r, zd_s, zd_r, a_r, b_r,
    sums, part_z, part_y,
    in_sem, send_sem, recv_sem,
    zs_sem, zr_sem, ys_sem, yr_sem,
):
    gy = lax.axis_index("gy")
    gz = lax.axis_index("gz")
    rows, depth, width = e_v.shape[1], e_v.shape[2], e_v.shape[3]

    pairs = (
        (e_in, e_v), (h_in, h_v), (q_in, q_v), (p_in, p_v), (n_in, n_v),
        (lab_in, lab_v), (gain_in, gain_v), (src_in, src_v), (es_in, es_v),
        (ns_in, ns_v), (hs_in, hs_v), (qs_in, qs_v), (ps_in, ps_v),
    )
    loads = [
        pltpu.make_async_copy(a, b, in_sem.at[i]) for i, (a, b) in enumerate(pairs)
    ]
    for copy in loads:
        copy.start()

    for ref in (yu_r, yd_r, zu_r, zd_r, a_r, b_r, zu_s, zd_s):
        ref[...] = jnp.zeros(ref.shape, ref.dtype)

    has_down, has_up = gy > 0, gy < ngy - 1
    has_left, has_right = gz > 0, gz < ngz - 1
    diag_a = jnp.logical_and(has_up, has_left)
    diag_b = jnp.logical_and(has_down, has_right)

    barrier = pltpu.get_barrier_semaphore()

    def greet_y(d, _):
        pl.semaphore_signal(
            barrier, inc=1, device_id=(lax.rem(gy + d, ngy), gz), device_id_type=MESH
        )
        return _

    def greet_z(d, _):
        pl.semaphore_signal(
            barrier, inc=1, device_id=(gy, lax.rem(gz + d, ngz)), device_id_type=MESH
        )
        return _

    lax.fori_loop(1, ngy, greet_y, 0)
    lax.fori_loop(1, ngz, greet_z, 0)

    @pl.when(diag_a)
    def _():
        pl.semaphore_signal(barrier, inc=1, device_id=(gy + 1, gz - 1), device_id_type=MESH)

    @pl.when(diag_b)
    def _():
        pl.semaphore_signal(barrier, inc=1, device_id=(gy - 1, gz + 1), device_id_type=MESH)

    def links(k):
        f = FIELDS[k]
        up = pl.ds(UP_AT[k], UP[k])
        down = pl.ds(DOWN_AT[k], DOWN[k])
        diag = pl.ds(DIAG_AT[k], f)
        return (
            (yu_s.at[up], yu_r.at[up], (gy + 1, gz), has_up, has_down),
            (yd_s.at[down], yd_r.at[down], (gy - 1, gz), has_down, has_up),
            (zu_s.at[up], zu_r.at[up], (gy, gz + 1), has_right, has_left),
            (zd_s.at[down], zd_r.at[down], (gy, gz - 1), has_left, has_right),
            (zd_s.at[pl.ds(DOWN_AT[k] + f, f)], a_r.at[diag], (gy + 1, gz - 1), diag_a, diag_b),
            (zu_s.at[pl.ds(UP_AT[k] + 2 * f, f)], b_r.at[diag], (gy - 1, gz + 1), diag_b, diag_a),
        )

    def remote(k, i, link):
        return pltpu.make_async_remote_copy(
            src_ref=link[0],
            dst_ref=link[1],
            send_sem=send_sem.at[k, i],
            recv_sem=recv_sem.at[k, i],
            device_id=link[2],
            device_id_type=MESH,
        )

    def send(k):
        for i, link in enumerate(links(k)):

            @pl.when(link[3])
            def _(i=i, link=link):
                remote(k, i, link).start()

    def receive(k):
        for i, link in enumerate(links(k)):

            @pl.when(link[4])
            def _(i=i, link=link):
                remote(k, i, link).wait_recv()

    def finish(k):
        for i, link in enumerate(links(k)):

            @pl.when(link[3])
            def _(i=i, link=link):
                remote(k, i, link).wait_send()

    tools = Shifts(depth, width)
    lane, tiles = tools.lane, tools.tiles
    widen, x_front, z_front = tools.widen, tools.x_front, tools.z_front
    group = math.gcd(rows, ROWS_PER_STEP)

    def curl_forward(ref, k, j, r):
        at = DOWN_AT[k] + j
        return tools.curl_forward(ref, zd_r[at], zd_r[at + FIELDS[k]], r, group)

    def block(ref, c, r):
        return ref[c, pl.ds(r, group)].astype(jnp.float32).reshape(group * depth, width)

    def flat(ref, r):
        return ref[pl.ds(r, group)].reshape(group * depth, width)

    def put(ref, c, r, value):
        ref[c, pl.ds(r, group)] = value.reshape(group, depth, width)

    def over_rows(body):
        def step(i, _):
            body(i * group)
            return _

        lax.fori_loop(0, rows // group, step, 0)

    def border_row(ref, k, j):
        f = FIELDS[k]
        vx, vy, vz = (yu_r[UP_AT[k] + c * f + j] for c in range(3))
        dz_y = z_front(vy, a_r[DIAG_AT[k] + j], rows - 1) - vy
        dy_x, dy_z = ref[0, 0] - vx, ref[2, 0] - vz
        return dy_z - dz_y, x_front(vy) - vy - dy_x

    def border_col(k, j):
        f = FIELDS[k]
        vx, vy, vz = (zu_r[UP_AT[k] + c * f + j] for c in range(3))
        corner = pltpu.roll(b_r[DIAG_AT[k] + j], rows - 1, 1)
        dy_z = jnp.where(lane == rows - 1, corner, pltpu.roll(vz, LANES - 1, 1)) - vz
        dz_x = zd_s[DOWN_AT[k] + j] - vx
        dz_y = zd_s[DOWN_AT[k] + f + j] - vy
        return dy_z - dz_y, dz_x - (x_front(vz) - vz)

    row_on = jnp.where(has_down, 1.0, 0.0).astype(jnp.float32)
    col_on = jnp.where(has_left, 1.0, 0.0).astype(jnp.float32)

    def pack(ref, slot, r, column):
        tile = ref[slot]
        for u in range(column.shape[0] // depth):
            part = jnp.broadcast_to(column[u * depth : (u + 1) * depth], (depth, LANES))
            tile = jnp.where(lane == r + u, part, tile)
        ref[slot] = tile

    def pack_first(k, j, r, vx, vy):
        f = FIELDS[k]
        pack(zd_s, DOWN_AT[k] + j, r, vx[:, :1])
        pack(zd_s, DOWN_AT[k] + f + j, r, vy[:, :1])

    def pack_last(k, j, r, values):
        f = FIELDS[k]
        for c, v in enumerate(values):
            pack(zu_s, UP_AT[k] + c * f + j, r, v[:, width - 1 :])

    def pack_base(k, r, vx, vy):
        pack(zu_s, UP_AT[k] + 3 * FIELDS[k], r, vx[:, width - 1 :])
        pack(zu_s, UP_AT[k] + 3 * FIELDS[k] + 1, r, vy[:, width - 1 :])

    def stage_rows(k, j, ref):
        f = FIELDS[k]
        for c in range(3):
            yu_s[UP_AT[k] + c * f + j] = ref[c, rows - 1]
        yd_s[DOWN_AT[k] + j] = ref[0, 0]
        yd_s[DOWN_AT[k] + f + j] = ref[2, 0]

    def take_rows(k, j, ref):
        f = FIELDS[k]
        ref[0, rows] = yd_r[DOWN_AT[k] + j]
        ref[2, rows] = yd_r[DOWN_AT[k] + f + j]

    loads[0].wait()
    loads[1].wait()

    def first_pass(r):
        v = [block(e_v, c, r) for c in range(3)]
        for c in range(3):
            put(ef, c, r, v[c])
        pack_first(0, 0, r, v[0], v[1])
        pack_last(0, 0, r, v)
        pack_base(0, r, block(h_v, 0, r), block(h_v, 1, r))

    over_rows(first_pass)
    stage_rows(0, 0, ef)
    yu_s[UP_AT[0] + 3] = h_v[0, rows - 1].astype(jnp.float32)
    yu_s[UP_AT[0] + 4] = h_v[2, rows - 1].astype(jnp.float32)

    greeted = (
        (ngy - 1) + (ngz - 1) + jnp.where(diag_a, 1, 0) + jnp.where(diag_b, 1, 0)
    )
    pl.semaphore_wait(barrier, greeted)
    send(0)

    begin = start[0].astype(jnp.float32)
    sine_first = jnp.sin(jnp.full((depth, LANES), SOURCE_OMEGA * begin, jnp.float32))
    sine_second = jnp.sin(jnp.full((depth, LANES), SOURCE_OMEGA * (begin + 1.0), jnp.float32))
    sine_first, sine_second = (
        jnp.concatenate([widen(v)] * group, axis=0) for v in (sine_first, sine_second)
    )

    for copy in loads[2:11]:
        copy.wait()

    def inverse_of(labels):
        value = jnp.full(labels.shape, table[0], jnp.float32)
        for label in range(1, count):
            value = jnp.where(labels == label, table[label], value)
        return value

    receive(0)
    take_rows(0, 0, ef)
    row_x, row_z = border_row(ef, 0, 0)
    m[0, 0] = row_on * (yu_r[UP_AT[0] + 3] - MAGNETIC_STEP * row_x)
    m[2, 0] = row_on * (yu_r[UP_AT[0] + 4] - MAGNETIC_STEP * row_z)
    col_x, col_y = border_col(0, 0)
    m_col[0] = col_on * (zu_r[UP_AT[0] + 3] - MAGNETIC_STEP * col_x)
    m_col[1] = col_on * (zu_r[UP_AT[0] + 4] - MAGNETIC_STEP * col_y)

    def forward_pass(r):
        curl = curl_forward(ef, 0, 0, r)
        mid = [block(h_v, c, r) - MAGNETIC_STEP * curl[c] for c in range(3)]
        c1 = tools.curl_backward(mid, m[0, r], m[2, r], m_col, r)
        for c in range(3):
            put(m, c, r + 1, mid[c])
        inverse = inverse_of(flat(lab_v, r))
        gain = flat(gain_v, r).astype(jnp.float32)
        source = flat(src_v, r)
        upper, lower = block(n_v, 0, r), block(n_v, 1, r)
        gain_c, gain_s = COUPLING * gain, STIMULATED * gain
        couple = gain_c * (upper - lower)
        nexts, rates, polars = [], [], []
        work = None
        for c in range(3):
            e, p, q = block(ef, c, r), block(p_v, c, r), block(q_v, c, r)
            rate = DAMPING * q - STIFFNESS * p + couple * e
            polars.append(p + TIME_STEP * rate)
            force = ELECTRIC_STEP * c1[c] - TIME_STEP * rate
            if c == 2:
                force = force - sine_first * source
            new = e + inverse * force
            put(q1, c, r, rate)
            put(f1, c, r, force)
            put(e1, c, r, new)
            work = new * rate if work is None else work + new * rate
            nexts.append(new)
            rates.append(rate)
        s = gain_s * work
        upper_1 = upper + TIME_STEP * (PUMPING * (1.0 - upper - lower) - UPPER_DECAY * upper) - s
        lower_1 = lower + TIME_STEP * (UPPER_DECAY * upper - LOWER_DECAY * lower) + s
        couple_1 = gain_c * (upper_1 - lower_1)
        k1[pl.ds(r, group)] = couple_1.reshape(group, depth, width)
        t2 = gain_s * (block(ns_v, 1, r) - block(ns_v, 0, r))
        half = ELECTRIC_STEP * inverse
        adj = []
        for c in range(3):
            rate = DAMPING * rates[c] - STIFFNESS * polars[c] + couple_1 * nexts[c]
            put(q2, c, r, rate)
            adj.append(half * (block(es_v, c, r) + t2 * rate))
            put(ac, c, r, adj[c])
        pack_first(1, 0, r, nexts[0], nexts[1])
        pack_last(1, 0, r, nexts)
        pack_first(1, 1, r, adj[0], adj[1])
        pack_last(1, 1, r, adj)
        pack_base(1, r, block(hs_v, 0, r), block(hs_v, 1, r))

    over_rows(forward_pass)

    stage_rows(1, 0, e1)
    stage_rows(1, 1, ac)
    yu_s[UP_AT[1] + 6] = hs_v[0, rows - 1]
    yu_s[UP_AT[1] + 7] = hs_v[2, rows - 1]
    send(1)
    for copy in loads[11:]:
        copy.wait()
    receive(1)
    take_rows(1, 0, e1)
    take_rows(1, 1, ac)
    row_x, row_z = border_row(e1, 1, 0)
    m[0, 0] = m[0, 0] - MAGNETIC_STEP * (row_on * row_x)
    m[2, 0] = m[2, 0] - MAGNETIC_STEP * (row_on * row_z)
    row_x, row_z = border_row(ac, 1, 1)
    hg[0, 0] = row_on * (yu_r[UP_AT[1] + 6] + row_x)
    hg[2, 0] = row_on * (yu_r[UP_AT[1] + 7] + row_z)
    col_x, col_y = border_col(1, 0)
    m_col[0] = m_col[0] - MAGNETIC_STEP * (col_on * col_x)
    m_col[1] = m_col[1] - MAGNETIC_STEP * (col_on * col_y)
    col_x, col_y = border_col(1, 1)
    b_col[0] = col_on * (zu_r[UP_AT[1] + 6] + col_x)
    b_col[1] = col_on * (zu_r[UP_AT[1] + 7] + col_y)
    sums[...] = jnp.zeros(sums.shape, jnp.float32)

    keep_upper = 1.0 - TIME_STEP * (PUMPING + UPPER_DECAY)
    feed_upper = TIME_STEP * UPPER_DECAY
    drain_lower = -TIME_STEP * PUMPING
    keep_lower = 1.0 - TIME_STEP * LOWER_DECAY

    def backward_pass(r):
        curl = curl_forward(e1, 1, 0, r)
        last = [block(m, c, r + 1) - MAGNETIC_STEP * curl[c] for c in range(3)]
        c2 = tools.curl_backward(last, m[0, r], m[2, r], m_col, r)
        put(m, 0, r + 1, last[0])
        put(m, 2, r + 1, last[2])
        curl = curl_forward(ac, 1, 1, r)
        hb = [block(hs_v, c, r) + curl[c] for c in range(3)]
        eb = tools.curl_backward(hb, hg[0, r], hg[2, r], b_col, r)
        for c in range(3):
            put(hg, c, r + 1, hb[c])

        labels = flat(lab_v, r)
        inverse = inverse_of(labels)
        gain = flat(gain_v, r).astype(jnp.float32)
        source = flat(src_v, r)
        gain_c, gain_s = COUPLING * gain, STIMULATED * gain
        seed_u, seed_l = block(ns_v, 0, r), block(ns_v, 1, r)
        t2 = gain_s * (seed_l - seed_u)
        couple_1 = flat(k1, r)
        total = None
        overlap = None
        b_e, a_p, a_q = [], [], []
        for c in range(3):
            e, rate = block(e1, c, r), block(q2, c, r)
            force = ELECTRIC_STEP * c2[c] - TIME_STEP * rate
            if c == 2:
                force = force - sine_second * source
            new = e + inverse * force
            adj_e = block(es_v, c, r) + t2 * rate
            term = adj_e * force
            total = term if total is None else total + term
            seed_p = block(ps_v, c, r)
            adj_q = block(qs_v, c, r) + t2 * new + TIME_STEP * (seed_p - inverse * adj_e)
            a_p.append(seed_p - STIFFNESS * adj_q)
            a_q.append(DAMPING * adj_q)
            b_e.append(adj_e + couple_1 * adj_q - MAGNETIC_STEP * eb[c])
            overlap = adj_q * e if overlap is None else overlap + adj_q * e
        bend = gain_c * overlap
        a_u = keep_upper * seed_u + feed_upper * seed_l + bend
        a_l = drain_lower * seed_u + keep_lower * seed_l - bend

        t1 = gain_s * (a_l - a_u)
        upper, lower = block(n_v, 0, r), block(n_v, 1, r)
        couple = gain_c * (upper - lower)
        overlap = None
        out = []
        for c in range(3):
            rate = block(q1, c, r)
            adj_e = b_e[c] + t1 * rate
            total = total + adj_e * block(f1, c, r)
            adj_f = inverse * adj_e
            curl_adj = ELECTRIC_STEP * adj_f
            out.append(curl_adj)
            put(cc, c, r, curl_adj)
            adj_q = a_q[c] + t1 * block(e1, c, r) + TIME_STEP * (a_p[c] - adj_f)
            put(pg, c, r, a_p[c] - STIFFNESS * adj_q)
            put(qg, c, r, DAMPING * adj_q)
            put(eg, c, r, adj_e + couple * adj_q)
            e = block(ef, c, r)
            overlap = adj_q * e if overlap is None else overlap + adj_q * e
        bend = gain_c * overlap
        put(ng, 0, r, keep_upper * a_u + feed_upper * a_l + bend)
        put(ng, 1, r, drain_lower * a_u + keep_lower * a_l - bend)
        cg[pl.ds(r, group)] = total.reshape(group, depth, width)
        for label in range(count):
            mine = jnp.where(labels == label, total, 0.0)
            sums[label] = sums[label] + sum(tools.rows_of(mine))
        pack_first(2, 0, r, out[0], out[1])
        pack_last(2, 0, r, out)

    over_rows(backward_pass)

    stage_rows(2, 0, cc)
    send(2)

    mine = jnp.zeros(part_z.shape[1:], jnp.float32)
    part_sub = lax.broadcasted_iota(jnp.int32, mine.shape, 0)
    for label in range(count):
        narrow = sum(sums[label, :, t * LANES : (t + 1) * LANES] for t in range(tiles))
        mine = jnp.where(part_sub == label, jnp.sum(narrow, axis=0, keepdims=True), mine)
    part_z[gz] = mine

    def gather(part, n, me, device, s_sem, r_sem):
        def copy_to(d):
            return pltpu.make_async_remote_copy(
                src_ref=part.at[me],
                dst_ref=part.at[me],
                send_sem=s_sem.at[d],
                recv_sem=r_sem.at[me],
                device_id=device(lax.rem(me + d, n)),
                device_id_type=MESH,
            )

        def copy_from(d):
            other = lax.rem(me + d, n)
            return pltpu.make_async_remote_copy(
                src_ref=part.at[other],
                dst_ref=part.at[other],
                send_sem=s_sem.at[d],
                recv_sem=r_sem.at[other],
                device_id=device(other),
                device_id_type=MESH,
            )

        def each(act):
            def body(d, _):
                act(d)
                return _

            lax.fori_loop(1, n, body, 0)

        return (
            lambda: each(lambda d: copy_to(d).start()),
            lambda: each(lambda d: copy_from(d).wait_recv()),
            lambda: each(lambda d: copy_to(d).wait_send()),
        )

    z_start, z_wait, z_sent = gather(part_z, ngz, gz, lambda o: (gy, o), zs_sem, zr_sem)
    y_start, y_wait, y_sent = gather(part_y, ngy, gy, lambda o: (o, gz), ys_sem, yr_sem)
    z_start()

    receive(2)
    take_rows(2, 0, cc)
    row_x, row_z = border_row(cc, 2, 0)
    hg[0, 0] = hg[0, 0] + row_on * row_x
    hg[2, 0] = hg[2, 0] + row_on * row_z
    col_x, col_y = border_col(2, 0)
    b_col[0] = b_col[0] + col_on * col_x
    b_col[1] = b_col[1] + col_on * col_y

    z_wait()
    part_y[gy] = jnp.sum(part_z[...], axis=0)
    y_start()
    tiles_out[0] = zd_r[DOWN_AT[2]]
    tiles_out[1] = zd_r[DOWN_AT[2] + 1]

    y_wait()
    whole = jnp.sum(part_y[...], axis=0)
    for label in range(count):
        tg_out[label] = jnp.sum(whole[label : label + 1, :]) * scale

    for k in range(3):
        finish(k)
    z_sent()
    y_sent()


def last_kernel(
    cc, hg, eg, pg, qg, ng, cg, tiles_in, b_col,
    eg_out, hg_out, pg_out, qg_out, ng_out, cg_out,
    hg_v, eg_v,
    sem, row_sem,
):
    rows, depth, width = cg.shape
    tools = Shifts(depth, width)
    group = math.gcd(rows, ROWS_PER_STEP)
    chunk = math.gcd(rows, 2 * group)
    size = group * depth
    ready = ((pg, pg_out), (qg, qg_out), (ng, ng_out), (cg, cg_out))
    copies = [pltpu.make_async_copy(a, b, sem.at[i]) for i, (a, b) in enumerate(ready)]
    for copy in copies:
        copy.start()
    hg_v[0, 0] = hg[0, 0]
    hg_v[2, 0] = hg[2, 0]

    def pass_rows(i, base):
        r = base + i * group
        curl = tools.curl_forward(cc, tiles_in[0], tiles_in[1], r, group)
        out = [
            hg[c, pl.ds(r + 1, group)].reshape(size, width) + curl[c] for c in range(3)
        ]
        back = tools.curl_backward(out, hg_v[0, r], hg_v[2, r], b_col, r)
        for c in range(3):
            hg_v[c, pl.ds(r + 1, group)] = out[c].reshape(group, depth, width)
            value = eg[c, pl.ds(r, group)].reshape(size, width) - MAGNETIC_STEP * back[c]
            eg_v[c, pl.ds(r, group)] = value.reshape(group, depth, width)
        return base

    for n, base in enumerate(range(0, rows, chunk)):
        lax.fori_loop(0, chunk // group, pass_rows, base)
        part = pl.ds(base, chunk)
        for i, (a, b) in enumerate(
            ((hg_v.at[:, pl.ds(base + 1, chunk)], hg_out.at[:, part]), (eg_v.at[:, part], eg_out.at[:, part]))
        ):
            copy = pltpu.make_async_copy(a, b, row_sem.at[n, i])
            copy.start()
            copies.append(copy)
    for copy in copies:
        copy.wait()


def solution(mesh):
    ngy, ngz = mesh.shape["gy"], mesh.shape["gz"]

    def on_device(*arrays):
        shape = arrays[0].shape
        _, rows, depth, width = shape
        count = arrays[12].shape[0]
        cells = rows * depth * width * ngy * ngz
        f32 = jnp.float32
        space = pl.BlockSpec(memory_space=pl.ANY)
        scalar = pl.BlockSpec(memory_space=pltpu.SMEM)
        three = jax.ShapeDtypeStruct(shape, f32)
        two = jax.ShapeDtypeStruct((2,) + shape[1:], f32)
        one = jax.ShapeDtypeStruct(shape[1:], f32)

        def vm(lead, wide=width):
            return pltpu.VMEM((lead, depth, wide), f32)

        def field(n, extra=0):
            return pltpu.VMEM((n, rows + extra, depth, width), f32)

        inputs = [
            pltpu.VMEM(arrays[i].shape, arrays[i].dtype) for i in (0, 1, 2, 3, 4, 5, 6, 7, 8, 9, 10, 11, 13)
        ]
        slots = -(-count // 8) * 8
        up, down, diag = sum(UP), sum(DOWN), sum(FIELDS)
        dma = pltpu.SemaphoreType.DMA
        scratch = inputs + [
            field(3, 1), field(3, 1), field(3, 1), field(3, 1),
            field(3), field(3), field(3), pltpu.VMEM(shape[1:], f32),
            vm(2, LANES),
            vm(up), vm(up), vm(down), vm(down),
            vm(up, LANES), vm(up, LANES), vm(down, LANES), vm(down, LANES),
            vm(diag, LANES), vm(diag, LANES),
            vm(count),
            pltpu.VMEM((ngz, slots, LANES), f32),
            pltpu.VMEM((ngy, slots, LANES), f32),
            dma((13,)), dma((3, 6)), dma((3, 6)),
            dma((ngz,)), dma((ngz,)), dma((ngy,)), dma((ngy,)),
        ]
        moved = 4 * rows * depth * width * 40
        kept = pl.BlockSpec(memory_space=pltpu.VMEM)
        *values, table = pl.pallas_call(
            functools.partial(kernel, ngy, ngz, count, 1.0 / math.sqrt(cells)),
            out_shape=(
                field(3, 1), field(3, 1), field(3), field(3), field(3), field(2),
                pltpu.VMEM(shape[1:], f32), vm(2, LANES), vm(2, LANES),
                jax.ShapeDtypeStruct((count,), f32),
            ),
            in_specs=[scalar if i in (12, 14) else space for i in range(15)],
            out_specs=(kept,) * 9 + (scalar,),
            scratch_shapes=scratch,
            cost_estimate=pl.CostEstimate(
                flops=500 * rows * depth * width, bytes_accessed=moved, transcendentals=0
            ),
            compiler_params=pltpu.CompilerParams(
                collective_id=0, has_side_effects=True, vmem_limit_bytes=58 * 1024 * 1024
            ),
        )(*arrays)
        group = math.gcd(rows, ROWS_PER_STEP)
        grads = pl.pallas_call(
            last_kernel,
            out_shape=(three, three, three, three, two, one),
            in_specs=[kept] * 9,
            out_specs=(space,) * 6,
            scratch_shapes=[
                field(3, 1), field(3), dma((4,)), dma((rows // math.gcd(rows, 2 * group), 2)),
            ],
            compiler_params=pltpu.CompilerParams(vmem_limit_bytes=24 * 1024 * 1024),
        )(*values)
        return (*grads, table)

    field = P(None, "gy", None, "gz")
    cell = P("gy", None, "gz")
    return jax.shard_map(
        on_device,
        mesh=mesh,
        in_specs=(field,) * 10 + (cell, cell, P(), cell, P()),
        out_specs=(field,) * 5 + (cell, P()),
        check_vma=False,
    )
```

```python
import functools
import math

import jax
import jax.numpy as jnp
from jax import lax
from jax.experimental import pallas as pl
from jax.experimental.pallas import tpu as pltpu
from jax.sharding import PartitionSpec as P

MAGNETIC_STEP = 0.5
ELECTRIC_STEP = 0.5
TIME_STEP = 0.5
DAMPING = 0.9
STIFFNESS = 0.3
COUPLING = 0.4
PUMPING = 0.05
UPPER_DECAY = 0.02
LOWER_DECAY = 0.3
STIMULATED = 0.2
SOURCE_OMEGA = 0.35

MESH = pl.DeviceIdType.MESH
LANES = 128
ROWS_PER_STEP = 4
FIELDS = (1, 2, 1)
BASES = (2, 2, 0)
UP = tuple(3 * f + b for f, b in zip(FIELDS, BASES))
DOWN = tuple(2 * f for f in FIELDS)
UP_AT = tuple(sum(UP[:k]) for k in range(3))
DOWN_AT = tuple(sum(DOWN[:k]) for k in range(3))
DIAG_AT = tuple(sum(FIELDS[:k]) for k in range(3))


class Shifts:
    def __init__(self, depth, width):
        self.depth, self.width, self.tiles = depth, width, width // LANES
        self.lane = lax.broadcasted_iota(jnp.int32, (depth, LANES), 1)

    def rows_of(self, v):
        return [v[u : u + self.depth] for u in range(0, v.shape[0], self.depth)]

    def widen(self, tile):
        return tile if self.tiles == 1 else jnp.concatenate([tile] * self.tiles, axis=1)

    def x_roll(self, v, shift, edge):
        s = lax.broadcasted_iota(jnp.int32, (self.depth, v.shape[1]), 0)
        rolled = [jnp.where(s == edge, 0.0, pltpu.roll(u, shift, 0)) for u in self.rows_of(v)]
        return jnp.concatenate(rolled, axis=0)

    def x_front(self, v):
        return self.x_roll(v, self.depth - 1, self.depth - 1)

    def x_behind(self, v):
        return self.x_roll(v, 1, 0)

    def z_front(self, v, tile, r):
        lanes = self.lane
        out = []
        for u, row in enumerate(self.rows_of(v)):
            border = pltpu.roll(tile, LANES - 1 - (r + u), 1)
            rolled = pltpu.roll(row, self.width - 1, 1)
            last = jnp.where(lanes == LANES - 1, border, rolled[:, self.width - LANES :])
            if self.tiles > 1:
                last = jnp.concatenate([rolled[:, : self.width - LANES], last], axis=1)
            out.append(last)
        return jnp.concatenate(out, axis=0)

    def z_behind(self, v, tile, r):
        lanes = self.lane
        out = []
        for u, row in enumerate(self.rows_of(v)):
            border = pltpu.roll(tile, lax.rem(LANES - (r + u), LANES), 1)
            rolled = pltpu.roll(row, 1, 1)
            first = jnp.where(lanes == 0, border, rolled[:, :LANES])
            if self.tiles > 1:
                first = jnp.concatenate([first, rolled[:, LANES:]], axis=1)
            out.append(first)
        return jnp.concatenate(out, axis=0)

    def curl_forward(self, ref, tile_x, tile_y, r, group):
        def load(c, at):
            return ref[c, pl.ds(at, group)].reshape(group * self.depth, self.width)

        vx, vy, vz = load(0, r), load(1, r), load(2, r)
        dy_x, dy_z = load(0, r + 1) - vx, load(2, r + 1) - vz
        dz_x = self.z_front(vx, tile_x, r) - vx
        dz_y = self.z_front(vy, tile_y, r) - vy
        dx_y, dx_z = self.x_front(vy) - vy, self.x_front(vz) - vz
        return (dy_z - dz_y, dz_x - dx_z, dx_y - dy_x)

    def curl_backward(self, v, back_x, back_z, col, r):
        vx, vy, vz = v

        def behind(row, whole):
            if whole.shape[0] == self.depth:
                return row
            return jnp.concatenate([row, whole[: -self.depth]], axis=0)

        dy_x, dy_z = vx - behind(back_x, vx), vz - behind(back_z, vz)
        dz_x = vx - self.z_behind(vx, col[0], r)
        dz_y = vy - self.z_behind(vy, col[1], r)
        dx_y, dx_z = vy - self.x_behind(vy), vz - self.x_behind(vz)
        return (dy_z - dz_y, dz_x - dx_z, dx_y - dy_x)


def kernel(
    ngy,
    ngz,
    count,
    e_in, h_in, p_in, q_in, n_in,
    es_in, hs_in, ps_in, qs_in, ns_in,
    lab_in, gain_in, table, src_in, start,
    cc, hg, eg, pg, qg, ng, cg, tiles_out, b_col, whole_out,
    e_v, h_v, p_v, q_v, n_v,
    es_v, hs_v, ps_v, qs_v, ns_v,
    lab_v, gain_v, src_v,
    ef, m, e1, ac, q1, q2, f1, k1,
    m_col,
    yu_s, yu_r, yd_s, yd_r, zu_s, zu_r, zd_s, zd_r, a_r, b_r,
    sums, part,
    in_sem, send_sem, recv_sem, part_sem,
):
    gy = lax.axis_index("gy")
    gz = lax.axis_index("gz")
    rows, depth, width = e_v.shape[1], e_v.shape[2], e_v.shape[3]

    pairs = (
        (e_in, e_v), (h_in, h_v), (q_in, q_v), (p_in, p_v), (n_in, n_v),
        (lab_in, lab_v), (gain_in, gain_v), (src_in, src_v), (es_in, es_v),
        (ns_in, ns_v), (hs_in, hs_v), (qs_in, qs_v), (ps_in, ps_v),
    )
    loads = [
        pltpu.make_async_copy(a, b, in_sem.at[i]) for i, (a, b) in enumerate(pairs)
    ]
    for copy in loads:
        copy.start()

    for ref in (yu_r, yd_r, zu_r, zd_r, a_r, b_r, zu_s, zd_s):
        ref[...] = jnp.zeros(ref.shape, ref.dtype)

    has_down, has_up = gy > 0, gy < ngy - 1
    has_left, has_right = gz > 0, gz < ngz - 1
    diag_a = jnp.logical_and(has_up, has_left)
    diag_b = jnp.logical_and(has_down, has_right)

    barrier = pltpu.get_barrier_semaphore()

    devices = ngy * ngz
    me = gy * ngz + gz

    def peer(d):
        other = lax.rem(me + d, devices)
        return (lax.div(other, ngz), lax.rem(other, ngz))

    def greet(d, _):
        pl.semaphore_signal(barrier, inc=1, device_id=peer(d), device_id_type=MESH)
        return _

    lax.fori_loop(1, devices, greet, 0)

    def links(k):
        f = FIELDS[k]
        up = pl.ds(UP_AT[k], UP[k])
        down = pl.ds(DOWN_AT[k], DOWN[k])
        diag = pl.ds(DIAG_AT[k], f)
        return (
            (yu_s.at[up], yu_r.at[up], (gy + 1, gz), has_up, has_down),
            (yd_s.at[down], yd_r.at[down], (gy - 1, gz), has_down, has_up),
            (zu_s.at[up], zu_r.at[up], (gy, gz + 1), has_right, has_left),
            (zd_s.at[down], zd_r.at[down], (gy, gz - 1), has_left, has_right),
            (zd_s.at[pl.ds(DOWN_AT[k] + f, f)], a_r.at[diag], (gy + 1, gz - 1), diag_a, diag_b),
            (zu_s.at[pl.ds(UP_AT[k] + 2 * f, f)], b_r.at[diag], (gy - 1, gz + 1), diag_b, diag_a),
        )

    def remote(k, i, link):
        return pltpu.make_async_remote_copy(
            src_ref=link[0],
            dst_ref=link[1],
            send_sem=send_sem.at[k, i],
            recv_sem=recv_sem.at[k, i],
            device_id=link[2],
            device_id_type=MESH,
        )

    def send(k):
        for i, link in enumerate(links(k)):

            @pl.when(link[3])
            def _(i=i, link=link):
                remote(k, i, link).start()

    def receive(k):
        for i, link in enumerate(links(k)):

            @pl.when(link[4])
            def _(i=i, link=link):
                remote(k, i, link).wait_recv()

    def finish(k):
        for i, link in enumerate(links(k)):

            @pl.when(link[3])
            def _(i=i, link=link):
                remote(k, i, link).wait_send()

    tools = Shifts(depth, width)
    lane, tiles = tools.lane, tools.tiles
    widen, x_front, z_front = tools.widen, tools.x_front, tools.z_front
    group = math.gcd(rows, ROWS_PER_STEP)

    def curl_forward(ref, k, j, r):
        at = DOWN_AT[k] + j
        return tools.curl_forward(ref, zd_r[at], zd_r[at + FIELDS[k]], r, group)

    def block(ref, c, r):
        return ref[c, pl.ds(r, group)].astype(jnp.float32).reshape(group * depth, width)

    def flat(ref, r):
        return ref[pl.ds(r, group)].reshape(group * depth, width)

    def put(ref, c, r, value):
        ref[c, pl.ds(r, group)] = value.reshape(group, depth, width)

    def over_rows(body):
        def step(i, _):
            body(i * group)
            return _

        lax.fori_loop(0, rows // group, step, 0)

    def border_row(ref, k, j):
        f = FIELDS[k]
        vx, vy, vz = (yu_r[UP_AT[k] + c * f + j] for c in range(3))
        dz_y = z_front(vy, a_r[DIAG_AT[k] + j], rows - 1) - vy
        dy_x, dy_z = ref[0, 0] - vx, ref[2, 0] - vz
        return dy_z - dz_y, x_front(vy) - vy - dy_x

    def border_col(k, j):
        f = FIELDS[k]
        vx, vy, vz = (zu_r[UP_AT[k] + c * f + j] for c in range(3))
        corner = pltpu.roll(b_r[DIAG_AT[k] + j], rows - 1, 1)
        dy_z = jnp.where(lane == rows - 1, corner, pltpu.roll(vz, LANES - 1, 1)) - vz
        dz_x = zd_s[DOWN_AT[k] + j] - vx
        dz_y = zd_s[DOWN_AT[k] + f + j] - vy
        return dy_z - dz_y, dz_x - (x_front(vz) - vz)

    row_on = jnp.where(has_down, 1.0, 0.0).astype(jnp.float32)
    col_on = jnp.where(has_left, 1.0, 0.0).astype(jnp.float32)

    def pack(ref, slot, r, column):
        tile = ref[slot]
        for u in range(column.shape[0] // depth):
            part = jnp.broadcast_to(column[u * depth : (u + 1) * depth], (depth, LANES))
            tile = jnp.where(lane == r + u, part, tile)
        ref[slot] = tile

    def pack_first(k, j, r, vx, vy):
        f = FIELDS[k]
        pack(zd_s, DOWN_AT[k] + j, r, vx[:, :1])
        pack(zd_s, DOWN_AT[k] + f + j, r, vy[:, :1])

    def pack_last(k, j, r, values):
        f = FIELDS[k]
        for c, v in enumerate(values):
            pack(zu_s, UP_AT[k] + c * f + j, r, v[:, width - 1 :])

    def pack_base(k, r, vx, vy):
        pack(zu_s, UP_AT[k] + 3 * FIELDS[k], r, vx[:, width - 1 :])
        pack(zu_s, UP_AT[k] + 3 * FIELDS[k] + 1, r, vy[:, width - 1 :])

    def stage_rows(k, j, ref):
        f = FIELDS[k]
        for c in range(3):
            yu_s[UP_AT[k] + c * f + j] = ref[c, rows - 1]
        yd_s[DOWN_AT[k] + j] = ref[0, 0]
        yd_s[DOWN_AT[k] + f + j] = ref[2, 0]

    def take_rows(k, j, ref):
        f = FIELDS[k]
        ref[0, rows] = yd_r[DOWN_AT[k] + j]
        ref[2, rows] = yd_r[DOWN_AT[k] + f + j]

    loads[0].wait()
    loads[1].wait()

    def first_pass(r):
        v = [block(e_v, c, r) for c in range(3)]
        for c in range(3):
            put(ef, c, r, v[c])
        pack_first(0, 0, r, v[0], v[1])
        pack_last(0, 0, r, v)
        pack_base(0, r, block(h_v, 0, r), block(h_v, 1, r))

    over_rows(first_pass)
    stage_rows(0, 0, ef)
    yu_s[UP_AT[0] + 3] = h_v[0, rows - 1].astype(jnp.float32)
    yu_s[UP_AT[0] + 4] = h_v[2, rows - 1].astype(jnp.float32)

    pl.semaphore_wait(barrier, devices - 1)
    send(0)

    begin = start[0].astype(jnp.float32)
    sine_first = jnp.sin(jnp.full((depth, LANES), SOURCE_OMEGA * begin, jnp.float32))
    sine_second = jnp.sin(jnp.full((depth, LANES), SOURCE_OMEGA * (begin + 1.0), jnp.float32))
    sine_first, sine_second = (
        jnp.concatenate([widen(v)] * group, axis=0) for v in (sine_first, sine_second)
    )

    for copy in loads[2:7]:
        copy.wait()

    def rate_pass(r):
        gain = flat(gain_v, r).astype(jnp.float32)
        couple = COUPLING * gain * (block(n_v, 0, r) - block(n_v, 1, r))
        for c in range(3):
            old = DAMPING * block(q_v, c, r) - STIFFNESS * block(p_v, c, r)
            put(q1, c, r, old + couple * block(ef, c, r))

    over_rows(rate_pass)
    for copy in loads[7:11]:
        copy.wait()

    def inverse_of(labels):
        value = jnp.full(labels.shape, table[0], jnp.float32)
        for label in range(1, count):
            value = jnp.where(labels == label, table[label], value)
        return value

    receive(0)
    take_rows(0, 0, ef)
    row_x, row_z = border_row(ef, 0, 0)
    m[0, 0] = row_on * (yu_r[UP_AT[0] + 3] - MAGNETIC_STEP * row_x)
    m[2, 0] = row_on * (yu_r[UP_AT[0] + 4] - MAGNETIC_STEP * row_z)
    col_x, col_y = border_col(0, 0)
    m_col[0] = col_on * (zu_r[UP_AT[0] + 3] - MAGNETIC_STEP * col_x)
    m_col[1] = col_on * (zu_r[UP_AT[0] + 4] - MAGNETIC_STEP * col_y)

    def forward_pass(r):
        curl = curl_forward(ef, 0, 0, r)
        mid = [block(h_v, c, r) - MAGNETIC_STEP * curl[c] for c in range(3)]
        c1 = tools.curl_backward(mid, m[0, r], m[2, r], m_col, r)
        for c in range(3):
            put(m, c, r + 1, mid[c])
        inverse = inverse_of(flat(lab_v, r))
        gain = flat(gain_v, r).astype(jnp.float32)
        source = flat(src_v, r)
        upper, lower = block(n_v, 0, r), block(n_v, 1, r)
        gain_c, gain_s = COUPLING * gain, STIMULATED * gain
        nexts, rates, polars = [], [], []
        work = None
        for c in range(3):
            e, rate = block(ef, c, r), block(q1, c, r)
            polars.append(block(p_v, c, r) + TIME_STEP * rate)
            force = ELECTRIC_STEP * c1[c] - TIME_STEP * rate
            if c == 2:
                force = force - sine_first * source
            new = e + inverse * force
            put(f1, c, r, force)
            put(e1, c, r, new)
            work = new * rate if work is None else work + new * rate
            nexts.append(new)
            rates.append(rate)
        s = gain_s * work
        upper_1 = upper + TIME_STEP * (PUMPING * (1.0 - upper - lower) - UPPER_DECAY * upper) - s
        lower_1 = lower + TIME_STEP * (UPPER_DECAY * upper - LOWER_DECAY * lower) + s
        couple_1 = gain_c * (upper_1 - lower_1)
        k1[pl.ds(r, group)] = couple_1.reshape(group, depth, width)
        t2 = gain_s * (block(ns_v, 1, r) - block(ns_v, 0, r))
        half = ELECTRIC_STEP * inverse
        adj = []
        for c in range(3):
            rate = DAMPING * rates[c] - STIFFNESS * polars[c] + couple_1 * nexts[c]
            put(q2, c, r, rate)
            adj.append(half * (block(es_v, c, r) + t2 * rate))
            put(ac, c, r, adj[c])
        pack_first(1, 0, r, nexts[0], nexts[1])
        pack_last(1, 0, r, nexts)
        pack_first(1, 1, r, adj[0], adj[1])
        pack_last(1, 1, r, adj)
        pack_base(1, r, block(hs_v, 0, r), block(hs_v, 1, r))

    over_rows(forward_pass)

    stage_rows(1, 0, e1)
    stage_rows(1, 1, ac)
    yu_s[UP_AT[1] + 6] = hs_v[0, rows - 1]
    yu_s[UP_AT[1] + 7] = hs_v[2, rows - 1]
    send(1)
    for copy in loads[11:]:
        copy.wait()

    def seed_pass(r):
        inverse = inverse_of(flat(lab_v, r))
        gain_s = STIMULATED * flat(gain_v, r).astype(jnp.float32)
        t2 = gain_s * (block(ns_v, 1, r) - block(ns_v, 0, r))
        total = None
        for c in range(3):
            rate = block(q2, c, r)
            force = -TIME_STEP * rate
            if c == 2:
                force = force - sine_second * flat(src_v, r)
            adj_e = block(es_v, c, r) + t2 * rate
            total = adj_e * force if total is None else total + adj_e * force
            new = block(e1, c, r) + inverse * force
            bent = TIME_STEP * (block(ps_v, c, r) - inverse * adj_e)
            put(qs_v, c, r, block(qs_v, c, r) + t2 * new + bent)
            put(es_v, c, r, adj_e)
        cg[pl.ds(r, group)] = total.reshape(group, depth, width)

    over_rows(seed_pass)
    receive(1)
    take_rows(1, 0, e1)
    take_rows(1, 1, ac)
    row_x, row_z = border_row(e1, 1, 0)
    m[0, 0] = m[0, 0] - MAGNETIC_STEP * (row_on * row_x)
    m[2, 0] = m[2, 0] - MAGNETIC_STEP * (row_on * row_z)
    row_x, row_z = border_row(ac, 1, 1)
    hg[0, 0] = row_on * (yu_r[UP_AT[1] + 6] + row_x)
    hg[2, 0] = row_on * (yu_r[UP_AT[1] + 7] + row_z)
    col_x, col_y = border_col(1, 0)
    m_col[0] = m_col[0] - MAGNETIC_STEP * (col_on * col_x)
    m_col[1] = m_col[1] - MAGNETIC_STEP * (col_on * col_y)
    col_x, col_y = border_col(1, 1)
    b_col[0] = col_on * (zu_r[UP_AT[1] + 6] + col_x)
    b_col[1] = col_on * (zu_r[UP_AT[1] + 7] + col_y)
    sums[...] = jnp.zeros(sums.shape, jnp.float32)

    keep_upper = 1.0 - TIME_STEP * (PUMPING + UPPER_DECAY)
    feed_upper = TIME_STEP * UPPER_DECAY
    drain_lower = -TIME_STEP * PUMPING
    keep_lower = 1.0 - TIME_STEP * LOWER_DECAY

    def backward_pass(r):
        curl = curl_forward(e1, 1, 0, r)
        last = [block(m, c, r + 1) - MAGNETIC_STEP * curl[c] for c in range(3)]
        c2 = tools.curl_backward(last, m[0, r], m[2, r], m_col, r)
        put(m, 0, r + 1, last[0])
        put(m, 2, r + 1, last[2])
        curl = curl_forward(ac, 1, 1, r)
        hb = [block(hs_v, c, r) + curl[c] for c in range(3)]
        eb = tools.curl_backward(hb, hg[0, r], hg[2, r], b_col, r)
        for c in range(3):
            put(hg, c, r + 1, hb[c])

        labels = flat(lab_v, r)
        inverse = inverse_of(labels)
        gain = flat(gain_v, r).astype(jnp.float32)
        gain_c, gain_s = COUPLING * gain, STIMULATED * gain
        seed_u, seed_l = block(ns_v, 0, r), block(ns_v, 1, r)
        t2 = gain_s * (seed_l - seed_u)
        couple_1 = flat(k1, r)
        total = flat(cg, r)
        overlap = None
        curl_t = ELECTRIC_STEP * t2 * inverse
        b_e, a_p, a_q = [], [], []
        for c in range(3):
            e = block(e1, c, r)
            adj_e = block(es_v, c, r)
            total = total + ELECTRIC_STEP * adj_e * c2[c]
            seed_p = block(ps_v, c, r)
            adj_q = block(qs_v, c, r) + curl_t * c2[c]
            a_p.append(seed_p - STIFFNESS * adj_q)
            a_q.append(DAMPING * adj_q)
            b_e.append(adj_e + couple_1 * adj_q - MAGNETIC_STEP * eb[c])
            overlap = adj_q * e if overlap is None else overlap + adj_q * e
        bend = gain_c * overlap
        a_u = keep_upper * seed_u + feed_upper * seed_l + bend
        a_l = drain_lower * seed_u + keep_lower * seed_l - bend

        t1 = gain_s * (a_l - a_u)
        upper, lower = block(n_v, 0, r), block(n_v, 1, r)
        couple = gain_c * (upper - lower)
        overlap = None
        out = []
        for c in range(3):
            rate = block(q1, c, r)
            adj_e = b_e[c] + t1 * rate
            total = total + adj_e * block(f1, c, r)
            adj_f = inverse * adj_e
            curl_adj = ELECTRIC_STEP * adj_f
            out.append(curl_adj)
            put(cc, c, r, curl_adj)
            adj_q = a_q[c] + t1 * block(e1, c, r) + TIME_STEP * (a_p[c] - adj_f)
            put(pg, c, r, a_p[c] - STIFFNESS * adj_q)
            put(qg, c, r, DAMPING * adj_q)
            put(eg, c, r, adj_e + couple * adj_q)
            e = block(ef, c, r)
            overlap = adj_q * e if overlap is None else overlap + adj_q * e
        bend = gain_c * overlap
        put(ng, 0, r, keep_upper * a_u + feed_upper * a_l + bend)
        put(ng, 1, r, drain_lower * a_u + keep_lower * a_l - bend)
        cg[pl.ds(r, group)] = total.reshape(group, depth, width)
        for label in range(count):
            mine = jnp.where(labels == label, total, 0.0)
            sums[label] = sums[label] + sum(tools.rows_of(mine))
        pack_first(2, 0, r, out[0], out[1])
        pack_last(2, 0, r, out)

    over_rows(backward_pass)

    stage_rows(2, 0, cc)
    send(2)

    mine = jnp.zeros(part.shape[1:], jnp.float32)
    part_sub = lax.broadcasted_iota(jnp.int32, mine.shape, 0)
    for label in range(count):
        narrow = sum(sums[label, :, t * LANES : (t + 1) * LANES] for t in range(tiles))
        mine = jnp.where(part_sub == label, jnp.sum(narrow, axis=0, keepdims=True), mine)
    part[me] = mine

    def part_copy(where, d):
        return pltpu.make_async_remote_copy(
            src_ref=part.at[where],
            dst_ref=part.at[where],
            send_sem=part_sem.at[0],
            recv_sem=part_sem.at[1],
            device_id=peer(d),
            device_id_type=MESH,
        )

    def part_send(d, _):
        part_copy(me, d).start()
        return _

    lax.fori_loop(1, devices, part_send, 0)
    others = part_copy(pl.ds(0, devices - 1), 1)

    receive(2)
    take_rows(2, 0, cc)
    row_x, row_z = border_row(cc, 2, 0)
    hg[0, 0] = hg[0, 0] + row_on * row_x
    hg[2, 0] = hg[2, 0] + row_on * row_z
    col_x, col_y = border_col(2, 0)
    b_col[0] = b_col[0] + col_on * col_x
    b_col[1] = b_col[1] + col_on * col_y

    tiles_out[0] = zd_r[DOWN_AT[2]]
    tiles_out[1] = zd_r[DOWN_AT[2] + 1]
    for k in range(3):
        finish(k)
    others.wait_recv()
    whole_out[...] = jnp.sum(part[...], axis=0)
    others.wait_send()


def last_kernel(
    scale,
    cc, hg, eg, pg, qg, ng, cg, tiles_in, b_col, whole,
    eg_out, hg_out, pg_out, qg_out, ng_out, cg_out, tg_out,
    hg_v, eg_v,
    sem, row_sem,
):
    rows, depth, width = cg.shape
    tools = Shifts(depth, width)
    group = math.gcd(rows, ROWS_PER_STEP)
    chunk = math.gcd(rows, 2 * group)
    size = group * depth
    ready = ((pg, pg_out), (qg, qg_out), (ng, ng_out), (cg, cg_out))
    copies = [pltpu.make_async_copy(a, b, sem.at[i]) for i, (a, b) in enumerate(ready)]
    for copy in copies:
        copy.start()
    for label in range(tg_out.shape[0]):
        tg_out[label] = jnp.sum(whole[label : label + 1, :]) * scale
    hg_v[0, 0] = hg[0, 0]
    hg_v[2, 0] = hg[2, 0]

    def pass_rows(i, base):
        r = base + i * group
        curl = tools.curl_forward(cc, tiles_in[0], tiles_in[1], r, group)
        out = [
            hg[c, pl.ds(r + 1, group)].reshape(size, width) + curl[c] for c in range(3)
        ]
        back = tools.curl_backward(out, hg_v[0, r], hg_v[2, r], b_col, r)
        for c in range(3):
            hg_v[c, pl.ds(r + 1, group)] = out[c].reshape(group, depth, width)
            value = eg[c, pl.ds(r, group)].reshape(size, width) - MAGNETIC_STEP * back[c]
            eg_v[c, pl.ds(r, group)] = value.reshape(group, depth, width)
        return base

    for n, base in enumerate(range(0, rows, chunk)):
        lax.fori_loop(0, chunk // group, pass_rows, base)
        part = pl.ds(base, chunk)
        for i, (a, b) in enumerate(
            ((hg_v.at[:, pl.ds(base + 1, chunk)], hg_out.at[:, part]), (eg_v.at[:, part], eg_out.at[:, part]))
        ):
            copy = pltpu.make_async_copy(a, b, row_sem.at[n, i])
            copy.start()
            copies.append(copy)
    for copy in copies:
        copy.wait()


def solution(mesh):
    ngy, ngz = mesh.shape["gy"], mesh.shape["gz"]

    def on_device(*arrays):
        shape = arrays[0].shape
        _, rows, depth, width = shape
        count = arrays[12].shape[0]
        cells = rows * depth * width * ngy * ngz
        f32 = jnp.float32
        space = pl.BlockSpec(memory_space=pl.ANY)
        scalar = pl.BlockSpec(memory_space=pltpu.SMEM)
        three = jax.ShapeDtypeStruct(shape, f32)
        two = jax.ShapeDtypeStruct((2,) + shape[1:], f32)
        one = jax.ShapeDtypeStruct(shape[1:], f32)

        def vm(lead, wide=width):
            return pltpu.VMEM((lead, depth, wide), f32)

        def field(n, extra=0):
            return pltpu.VMEM((n, rows + extra, depth, width), f32)

        inputs = [
            pltpu.VMEM(arrays[i].shape, arrays[i].dtype) for i in (0, 1, 2, 3, 4, 5, 6, 7, 8, 9, 10, 11, 13)
        ]
        slots = -(-count // 8) * 8
        up, down, diag = sum(UP), sum(DOWN), sum(FIELDS)
        dma = pltpu.SemaphoreType.DMA
        scratch = inputs + [
            field(3, 1), field(3, 1), field(3, 1), field(3, 1),
            field(3), field(3), field(3), pltpu.VMEM(shape[1:], f32),
            vm(2, LANES),
            vm(up), vm(up), vm(down), vm(down),
            vm(up, LANES), vm(up, LANES), vm(down, LANES), vm(down, LANES),
            vm(diag, LANES), vm(diag, LANES),
            vm(count),
            pltpu.VMEM((ngy * ngz, slots, LANES), f32),
            dma((13,)), dma((3, 6)), dma((3, 6)), dma((2,)),
        ]
        moved = 4 * rows * depth * width * 40
        kept = pl.BlockSpec(memory_space=pltpu.VMEM)
        values = pl.pallas_call(
            functools.partial(kernel, ngy, ngz, count),
            out_shape=(
                field(3, 1), field(3, 1), field(3), field(3), field(3), field(2),
                pltpu.VMEM(shape[1:], f32), vm(2, LANES), vm(2, LANES),
                pltpu.VMEM((slots, LANES), f32),
            ),
            in_specs=[scalar if i in (12, 14) else space for i in range(15)],
            out_specs=(kept,) * 10,
            scratch_shapes=scratch,
            cost_estimate=pl.CostEstimate(
                flops=500 * rows * depth * width, bytes_accessed=moved, transcendentals=0
            ),
            compiler_params=pltpu.CompilerParams(
                collective_id=0, has_side_effects=True, vmem_limit_bytes=58 * 1024 * 1024
            ),
        )(*arrays)
        group = math.gcd(rows, ROWS_PER_STEP)
        table = jax.ShapeDtypeStruct((count,), f32)
        return pl.pallas_call(
            functools.partial(last_kernel, 1.0 / math.sqrt(cells)),
            out_shape=(three, three, three, three, two, one, table),
            in_specs=[kept] * 10,
            out_specs=(space,) * 6 + (scalar,),
            scratch_shapes=[
                field(3, 1), field(3), dma((4,)), dma((rows // math.gcd(rows, 2 * group), 2)),
            ],
            compiler_params=pltpu.CompilerParams(vmem_limit_bytes=24 * 1024 * 1024),
        )(*values)

    field = P(None, "gy", None, "gz")
    cell = P("gy", None, "gz")
    return jax.shard_map(
        on_device,
        mesh=mesh,
        in_specs=(field,) * 10 + (cell, cell, P(), cell, P()),
        out_specs=(field,) * 5 + (cell, P()),
        check_vma=False,
    )
```

```python
import functools
import math

import jax
import jax.numpy as jnp
from jax import lax
from jax.experimental import pallas as pl
from jax.experimental.pallas import tpu as pltpu
from jax.sharding import PartitionSpec as P

MAGNETIC_STEP = 0.5
ELECTRIC_STEP = 0.5
TIME_STEP = 0.5
DAMPING = 0.9
STIFFNESS = 0.3
COUPLING = 0.4
PUMPING = 0.05
UPPER_DECAY = 0.02
LOWER_DECAY = 0.3
STIMULATED = 0.2
SOURCE_OMEGA = 0.35

MESH = pl.DeviceIdType.MESH
LANES = 128
ROWS_PER_STEP = 4
FIELDS = (1, 2, 1)
BASES = (2, 2, 0)
UP = tuple(3 * f + b for f, b in zip(FIELDS, BASES))
DOWN = tuple(2 * f for f in FIELDS)
UP_AT = tuple(sum(UP[:k]) for k in range(3))
DOWN_AT = tuple(sum(DOWN[:k]) for k in range(3))
DIAG_AT = tuple(sum(FIELDS[:k]) for k in range(3))


class Shifts:
    def __init__(self, depth, width):
        self.depth, self.width, self.tiles = depth, width, width // LANES
        self.lane = lax.broadcasted_iota(jnp.int32, (depth, LANES), 1)

    def rows_of(self, v):
        return [v[u : u + self.depth] for u in range(0, v.shape[0], self.depth)]

    def widen(self, tile):
        return tile if self.tiles == 1 else jnp.concatenate([tile] * self.tiles, axis=1)

    def x_roll(self, v, shift, edge):
        s = lax.broadcasted_iota(jnp.int32, (self.depth, v.shape[1]), 0)
        rolled = [jnp.where(s == edge, 0.0, pltpu.roll(u, shift, 0)) for u in self.rows_of(v)]
        return jnp.concatenate(rolled, axis=0)

    def x_front(self, v):
        return self.x_roll(v, self.depth - 1, self.depth - 1)

    def x_behind(self, v):
        return self.x_roll(v, 1, 0)

    def z_front(self, v, tile, r):
        lanes = self.lane
        out = []
        for u, row in enumerate(self.rows_of(v)):
            border = pltpu.roll(tile, LANES - 1 - (r + u), 1)
            rolled = pltpu.roll(row, self.width - 1, 1)
            last = jnp.where(lanes == LANES - 1, border, rolled[:, self.width - LANES :])
            if self.tiles > 1:
                last = jnp.concatenate([rolled[:, : self.width - LANES], last], axis=1)
            out.append(last)
        return jnp.concatenate(out, axis=0)

    def z_behind(self, v, tile, r):
        lanes = self.lane
        out = []
        for u, row in enumerate(self.rows_of(v)):
            border = pltpu.roll(tile, lax.rem(LANES - (r + u), LANES), 1)
            rolled = pltpu.roll(row, 1, 1)
            first = jnp.where(lanes == 0, border, rolled[:, :LANES])
            if self.tiles > 1:
                first = jnp.concatenate([first, rolled[:, LANES:]], axis=1)
            out.append(first)
        return jnp.concatenate(out, axis=0)

    def curl_forward(self, ref, tile_x, tile_y, r, group):
        def load(c, at):
            return ref[c, pl.ds(at, group)].reshape(group * self.depth, self.width)

        vx, vy, vz = load(0, r), load(1, r), load(2, r)
        dy_x, dy_z = load(0, r + 1) - vx, load(2, r + 1) - vz
        dz_x = self.z_front(vx, tile_x, r) - vx
        dz_y = self.z_front(vy, tile_y, r) - vy
        dx_y, dx_z = self.x_front(vy) - vy, self.x_front(vz) - vz
        return (dy_z - dz_y, dz_x - dx_z, dx_y - dy_x)

    def curl_backward(self, v, back_x, back_z, col, r):
        vx, vy, vz = v

        def behind(row, whole):
            if whole.shape[0] == self.depth:
                return row
            return jnp.concatenate([row, whole[: -self.depth]], axis=0)

        dy_x, dy_z = vx - behind(back_x, vx), vz - behind(back_z, vz)
        dz_x = vx - self.z_behind(vx, col[0], r)
        dz_y = vy - self.z_behind(vy, col[1], r)
        dx_y, dx_z = vy - self.x_behind(vy), vz - self.x_behind(vz)
        return (dy_z - dz_y, dz_x - dx_z, dx_y - dy_x)


def kernel(
    ngy,
    ngz,
    count,
    e_in, h_in, p_in, q_in, n_in,
    es_in, hs_in, ps_in, qs_in, ns_in,
    lab_in, gain_in, table, src_in, start,
    cc, hg, eg, pg, qg, ng, cg, tiles_out, b_col, whole_out,
    e_v, h_v, p_v, q_v, n_v,
    es_v, hs_v, ps_v, qs_v, ns_v,
    lab_v, gain_v, src_v,
    ef, m, e1, ac, q1, q2, f1, k1,
    m_col,
    yu_s, yu_r, yd_s, yd_r, zu_s, zu_r, zd_s, zd_r, a_r, b_r,
    sums, part,
    in_sem, send_sem, recv_sem, part_sem,
):
    gy = lax.axis_index("gy")
    gz = lax.axis_index("gz")
    rows, depth, width = e_v.shape[1], e_v.shape[2], e_v.shape[3]

    pairs = (
        (e_in, e_v), (h_in, h_v), (q_in, q_v), (p_in, p_v), (n_in, n_v),
        (lab_in, lab_v), (gain_in, gain_v), (src_in, src_v), (es_in, es_v),
        (ns_in, ns_v), (hs_in, hs_v), (qs_in, qs_v), (ps_in, ps_v),
    )
    loads = [
        pltpu.make_async_copy(a, b, in_sem.at[i]) for i, (a, b) in enumerate(pairs)
    ]
    for copy in loads[:2]:
        copy.start()

    for ref in (yu_r, yd_r, zu_r, zd_r, a_r, b_r, zu_s, zd_s):
        ref[...] = jnp.zeros(ref.shape, ref.dtype)

    has_down, has_up = gy > 0, gy < ngy - 1
    has_left, has_right = gz > 0, gz < ngz - 1
    diag_a = jnp.logical_and(has_up, has_left)
    diag_b = jnp.logical_and(has_down, has_right)

    barrier = pltpu.get_barrier_semaphore()

    devices = ngy * ngz
    me = gy * ngz + gz

    def peer(d):
        other = lax.rem(me + d, devices)
        return (lax.div(other, ngz), lax.rem(other, ngz))

    def greet(d, _):
        pl.semaphore_signal(barrier, inc=1, device_id=peer(d), device_id_type=MESH)
        return _

    lax.fori_loop(1, devices, greet, 0)

    def links(k):
        f = FIELDS[k]
        up = pl.ds(UP_AT[k], UP[k])
        down = pl.ds(DOWN_AT[k], DOWN[k])
        diag = pl.ds(DIAG_AT[k], f)
        return (
            (yu_s.at[up], yu_r.at[up], (gy + 1, gz), has_up, has_down),
            (yd_s.at[down], yd_r.at[down], (gy - 1, gz), has_down, has_up),
            (zu_s.at[up], zu_r.at[up], (gy, gz + 1), has_right, has_left),
            (zd_s.at[down], zd_r.at[down], (gy, gz - 1), has_left, has_right),
            (zd_s.at[pl.ds(DOWN_AT[k] + f, f)], a_r.at[diag], (gy + 1, gz - 1), diag_a, diag_b),
            (zu_s.at[pl.ds(UP_AT[k] + 2 * f, f)], b_r.at[diag], (gy - 1, gz + 1), diag_b, diag_a),
        )

    def remote(k, i, link):
        return pltpu.make_async_remote_copy(
            src_ref=link[0],
            dst_ref=link[1],
            send_sem=send_sem.at[k, i],
            recv_sem=recv_sem.at[k, i],
            device_id=link[2],
            device_id_type=MESH,
        )

    def send(k):
        for i, link in enumerate(links(k)):

            @pl.when(link[3])
            def _(i=i, link=link):
                remote(k, i, link).start()

    def receive(k):
        for i, link in enumerate(links(k)):

            @pl.when(link[4])
            def _(i=i, link=link):
                remote(k, i, link).wait_recv()

    def finish(k):
        for i, link in enumerate(links(k)):

            @pl.when(link[3])
            def _(i=i, link=link):
                remote(k, i, link).wait_send()

    tools = Shifts(depth, width)
    lane, tiles = tools.lane, tools.tiles
    widen, x_front, z_front = tools.widen, tools.x_front, tools.z_front
    group = math.gcd(rows, ROWS_PER_STEP)

    def curl_forward(ref, k, j, r):
        at = DOWN_AT[k] + j
        return tools.curl_forward(ref, zd_r[at], zd_r[at + FIELDS[k]], r, group)

    def block(ref, c, r):
        return ref[c, pl.ds(r, group)].astype(jnp.float32).reshape(group * depth, width)

    def flat(ref, r):
        return ref[pl.ds(r, group)].reshape(group * depth, width)

    def put(ref, c, r, value):
        ref[c, pl.ds(r, group)] = value.reshape(group, depth, width)

    def over_rows(body):
        def step(i, _):
            body(i * group)
            return _

        lax.fori_loop(0, rows // group, step, 0)

    def border_row(ref, k, j):
        f = FIELDS[k]
        vx, vy, vz = (yu_r[UP_AT[k] + c * f + j] for c in range(3))
        dz_y = z_front(vy, a_r[DIAG_AT[k] + j], rows - 1) - vy
        dy_x, dy_z = ref[0, 0] - vx, ref[2, 0] - vz
        return dy_z - dz_y, x_front(vy) - vy - dy_x

    def border_col(k, j):
        f = FIELDS[k]
        vx, vy, vz = (zu_r[UP_AT[k] + c * f + j] for c in range(3))
        corner = pltpu.roll(b_r[DIAG_AT[k] + j], rows - 1, 1)
        dy_z = jnp.where(lane == rows - 1, corner, pltpu.roll(vz, LANES - 1, 1)) - vz
        dz_x = zd_s[DOWN_AT[k] + j] - vx
        dz_y = zd_s[DOWN_AT[k] + f + j] - vy
        return dy_z - dz_y, dz_x - (x_front(vz) - vz)

    row_on = jnp.where(has_down, 1.0, 0.0).astype(jnp.float32)
    col_on = jnp.where(has_left, 1.0, 0.0).astype(jnp.float32)

    def pack(ref, slot, r, column):
        tile = ref[slot]
        for u in range(column.shape[0] // depth):
            part = jnp.broadcast_to(column[u * depth : (u + 1) * depth], (depth, LANES))
            tile = jnp.where(lane == r + u, part, tile)
        ref[slot] = tile

    def pack_first(k, j, r, vx, vy):
        f = FIELDS[k]
        pack(zd_s, DOWN_AT[k] + j, r, vx[:, :1])
        pack(zd_s, DOWN_AT[k] + f + j, r, vy[:, :1])

    def pack_last(k, j, r, values):
        f = FIELDS[k]
        for c, v in enumerate(values):
            pack(zu_s, UP_AT[k] + c * f + j, r, v[:, width - 1 :])

    def pack_base(k, r, vx, vy):
        pack(zu_s, UP_AT[k] + 3 * FIELDS[k], r, vx[:, width - 1 :])
        pack(zu_s, UP_AT[k] + 3 * FIELDS[k] + 1, r, vy[:, width - 1 :])

    def stage_rows(k, j, ref):
        f = FIELDS[k]
        for c in range(3):
            yu_s[UP_AT[k] + c * f + j] = ref[c, rows - 1]
        yd_s[DOWN_AT[k] + j] = ref[0, 0]
        yd_s[DOWN_AT[k] + f + j] = ref[2, 0]

    def take_rows(k, j, ref):
        f = FIELDS[k]
        ref[0, rows] = yd_r[DOWN_AT[k] + j]
        ref[2, rows] = yd_r[DOWN_AT[k] + f + j]

    loads[0].wait()
    loads[1].wait()
    for copy in loads[2:]:
        copy.start()

    def first_pass(r):
        v = [block(e_v, c, r) for c in range(3)]
        for c in range(3):
            put(ef, c, r, v[c])
        pack_first(0, 0, r, v[0], v[1])
        pack_last(0, 0, r, v)
        pack_base(0, r, block(h_v, 0, r), block(h_v, 1, r))

    over_rows(first_pass)
    stage_rows(0, 0, ef)
    yu_s[UP_AT[0] + 3] = h_v[0, rows - 1].astype(jnp.float32)
    yu_s[UP_AT[0] + 4] = h_v[2, rows - 1].astype(jnp.float32)

    pl.semaphore_wait(barrier, devices - 1)
    send(0)

    begin = start[0].astype(jnp.float32)
    sine_first = jnp.sin(jnp.full((depth, LANES), SOURCE_OMEGA * begin, jnp.float32))
    sine_second = jnp.sin(jnp.full((depth, LANES), SOURCE_OMEGA * (begin + 1.0), jnp.float32))
    sine_first, sine_second = (
        jnp.concatenate([widen(v)] * group, axis=0) for v in (sine_first, sine_second)
    )

    for copy in loads[2:7]:
        copy.wait()

    def rate_pass(r):
        gain = flat(gain_v, r).astype(jnp.float32)
        couple = COUPLING * gain * (block(n_v, 0, r) - block(n_v, 1, r))
        for c in range(3):
            old = DAMPING * block(q_v, c, r) - STIFFNESS * block(p_v, c, r)
            put(q1, c, r, old + couple * block(ef, c, r))

    over_rows(rate_pass)
    for copy in loads[7:11]:
        copy.wait()

    def inverse_of(labels):
        value = jnp.full(labels.shape, table[0], jnp.float32)
        for label in range(1, count):
            value = jnp.where(labels == label, table[label], value)
        return value

    receive(0)
    take_rows(0, 0, ef)
    row_x, row_z = border_row(ef, 0, 0)
    m[0, 0] = row_on * (yu_r[UP_AT[0] + 3] - MAGNETIC_STEP * row_x)
    m[2, 0] = row_on * (yu_r[UP_AT[0] + 4] - MAGNETIC_STEP * row_z)
    col_x, col_y = border_col(0, 0)
    m_col[0] = col_on * (zu_r[UP_AT[0] + 3] - MAGNETIC_STEP * col_x)
    m_col[1] = col_on * (zu_r[UP_AT[0] + 4] - MAGNETIC_STEP * col_y)

    def forward_pass(r):
        curl = curl_forward(ef, 0, 0, r)
        mid = [block(h_v, c, r) - MAGNETIC_STEP * curl[c] for c in range(3)]
        c1 = tools.curl_backward(mid, m[0, r], m[2, r], m_col, r)
        for c in range(3):
            put(m, c, r + 1, mid[c])
        inverse = inverse_of(flat(lab_v, r))
        gain = flat(gain_v, r).astype(jnp.float32)
        source = flat(src_v, r)
        upper, lower = block(n_v, 0, r), block(n_v, 1, r)
        gain_c, gain_s = COUPLING * gain, STIMULATED * gain
        nexts, rates, polars = [], [], []
        work = None
        for c in range(3):
            e, rate = block(ef, c, r), block(q1, c, r)
            polars.append(block(p_v, c, r) + TIME_STEP * rate)
            force = ELECTRIC_STEP * c1[c] - TIME_STEP * rate
            if c == 2:
                force = force - sine_first * source
            new = e + inverse * force
            put(f1, c, r, force)
            put(e1, c, r, new)
            work = new * rate if work is None else work + new * rate
            nexts.append(new)
            rates.append(rate)
        s = gain_s * work
        upper_1 = upper + TIME_STEP * (PUMPING * (1.0 - upper - lower) - UPPER_DECAY * upper) - s
        lower_1 = lower + TIME_STEP * (UPPER_DECAY * upper - LOWER_DECAY * lower) + s
        couple_1 = gain_c * (upper_1 - lower_1)
        k1[pl.ds(r, group)] = couple_1.reshape(group, depth, width)
        t2 = gain_s * (block(ns_v, 1, r) - block(ns_v, 0, r))
        half = ELECTRIC_STEP * inverse
        adj = []
        for c in range(3):
            rate = DAMPING * rates[c] - STIFFNESS * polars[c] + couple_1 * nexts[c]
            put(q2, c, r, rate)
            adj.append(half * (block(es_v, c, r) + t2 * rate))
            put(ac, c, r, adj[c])
        pack_first(1, 0, r, nexts[0], nexts[1])
        pack_last(1, 0, r, nexts)
        pack_first(1, 1, r, adj[0], adj[1])
        pack_last(1, 1, r, adj)
        pack_base(1, r, block(hs_v, 0, r), block(hs_v, 1, r))

    over_rows(forward_pass)

    stage_rows(1, 0, e1)
    stage_rows(1, 1, ac)
    yu_s[UP_AT[1] + 6] = hs_v[0, rows - 1]
    yu_s[UP_AT[1] + 7] = hs_v[2, rows - 1]
    send(1)
    for copy in loads[11:]:
        copy.wait()

    def seed_pass(r):
        inverse = inverse_of(flat(lab_v, r))
        gain_s = STIMULATED * flat(gain_v, r).astype(jnp.float32)
        t2 = gain_s * (block(ns_v, 1, r) - block(ns_v, 0, r))
        total = None
        for c in range(3):
            rate = block(q2, c, r)
            force = -TIME_STEP * rate
            if c == 2:
                force = force - sine_second * flat(src_v, r)
            adj_e = block(es_v, c, r) + t2 * rate
            total = adj_e * force if total is None else total + adj_e * force
            new = block(e1, c, r) + inverse * force
            bent = TIME_STEP * (block(ps_v, c, r) - inverse * adj_e)
            put(qs_v, c, r, block(qs_v, c, r) + t2 * new + bent)
            put(es_v, c, r, adj_e)
        cg[pl.ds(r, group)] = total.reshape(group, depth, width)

    over_rows(seed_pass)
    receive(1)
    take_rows(1, 0, e1)
    take_rows(1, 1, ac)
    row_x, row_z = border_row(e1, 1, 0)
    m[0, 0] = m[0, 0] - MAGNETIC_STEP * (row_on * row_x)
    m[2, 0] = m[2, 0] - MAGNETIC_STEP * (row_on * row_z)
    row_x, row_z = border_row(ac, 1, 1)
    hg[0, 0] = row_on * (yu_r[UP_AT[1] + 6] + row_x)
    hg[2, 0] = row_on * (yu_r[UP_AT[1] + 7] + row_z)
    col_x, col_y = border_col(1, 0)
    m_col[0] = m_col[0] - MAGNETIC_STEP * (col_on * col_x)
    m_col[1] = m_col[1] - MAGNETIC_STEP * (col_on * col_y)
    col_x, col_y = border_col(1, 1)
    b_col[0] = col_on * (zu_r[UP_AT[1] + 6] + col_x)
    b_col[1] = col_on * (zu_r[UP_AT[1] + 7] + col_y)
    sums[...] = jnp.zeros(sums.shape, jnp.float32)

    keep_upper = 1.0 - TIME_STEP * (PUMPING + UPPER_DECAY)
    feed_upper = TIME_STEP * UPPER_DECAY
    drain_lower = -TIME_STEP * PUMPING
    keep_lower = 1.0 - TIME_STEP * LOWER_DECAY

    def backward_pass(r):
        curl = curl_forward(e1, 1, 0, r)
        last = [block(m, c, r + 1) - MAGNETIC_STEP * curl[c] for c in range(3)]
        c2 = tools.curl_backward(last, m[0, r], m[2, r], m_col, r)
        put(m, 0, r + 1, last[0])
        put(m, 2, r + 1, last[2])
        curl = curl_forward(ac, 1, 1, r)
        hb = [block(hs_v, c, r) + curl[c] for c in range(3)]
        eb = tools.curl_backward(hb, hg[0, r], hg[2, r], b_col, r)
        for c in range(3):
            put(hg, c, r + 1, hb[c])

        labels = flat(lab_v, r)
        inverse = inverse_of(labels)
        gain = flat(gain_v, r).astype(jnp.float32)
        gain_c, gain_s = COUPLING * gain, STIMULATED * gain
        seed_u, seed_l = block(ns_v, 0, r), block(ns_v, 1, r)
        t2 = gain_s * (seed_l - seed_u)
        couple_1 = flat(k1, r)
        total = flat(cg, r)
        overlap = None
        curl_t = ELECTRIC_STEP * t2 * inverse
        b_e, a_p, a_q = [], [], []
        for c in range(3):
            e = block(e1, c, r)
            adj_e = block(es_v, c, r)
            total = total + ELECTRIC_STEP * adj_e * c2[c]
            seed_p = block(ps_v, c, r)
            adj_q = block(qs_v, c, r) + curl_t * c2[c]
            a_p.append(seed_p - STIFFNESS * adj_q)
            a_q.append(DAMPING * adj_q)
            b_e.append(adj_e + couple_1 * adj_q - MAGNETIC_STEP * eb[c])
            overlap = adj_q * e if overlap is None else overlap + adj_q * e
        bend = gain_c * overlap
        a_u = keep_upper * seed_u + feed_upper * seed_l + bend
        a_l = drain_lower * seed_u + keep_lower * seed_l - bend

        t1 = gain_s * (a_l - a_u)
        upper, lower = block(n_v, 0, r), block(n_v, 1, r)
        couple = gain_c * (upper - lower)
        overlap = None
        out = []
        for c in range(3):
            rate = block(q1, c, r)
            adj_e = b_e[c] + t1 * rate
            total = total + adj_e * block(f1, c, r)
            adj_f = inverse * adj_e
            curl_adj = ELECTRIC_STEP * adj_f
            out.append(curl_adj)
            put(cc, c, r, curl_adj)
            adj_q = a_q[c] + t1 * block(e1, c, r) + TIME_STEP * (a_p[c] - adj_f)
            put(pg, c, r, a_p[c] - STIFFNESS * adj_q)
            put(qg, c, r, DAMPING * adj_q)
            put(eg, c, r, adj_e + couple * adj_q)
            e = block(ef, c, r)
            overlap = adj_q * e if overlap is None else overlap + adj_q * e
        bend = gain_c * overlap
        put(ng, 0, r, keep_upper * a_u + feed_upper * a_l + bend)
        put(ng, 1, r, drain_lower * a_u + keep_lower * a_l - bend)
        cg[pl.ds(r, group)] = total.reshape(group, depth, width)
        for label in range(count):
            mine = jnp.where(labels == label, total, 0.0)
            sums[label] = sums[label] + sum(tools.rows_of(mine))
        pack_first(2, 0, r, out[0], out[1])
        pack_last(2, 0, r, out)

    over_rows(backward_pass)

    stage_rows(2, 0, cc)
    send(2)

    mine = jnp.zeros(part.shape[1:], jnp.float32)
    part_sub = lax.broadcasted_iota(jnp.int32, mine.shape, 0)
    for label in range(count):
        narrow = sum(sums[label, :, t * LANES : (t + 1) * LANES] for t in range(tiles))
        mine = jnp.where(part_sub == label, jnp.sum(narrow, axis=0, keepdims=True), mine)
    part[me] = mine

    def part_copy(where, d):
        return pltpu.make_async_remote_copy(
            src_ref=part.at[where],
            dst_ref=part.at[where],
            send_sem=part_sem.at[0],
            recv_sem=part_sem.at[1],
            device_id=peer(d),
            device_id_type=MESH,
        )

    def part_send(d, _):
        part_copy(me, d).start()
        return _

    lax.fori_loop(1, devices, part_send, 0)
    others = part_copy(pl.ds(0, devices - 1), 1)

    receive(2)
    take_rows(2, 0, cc)
    row_x, row_z = border_row(cc, 2, 0)
    hg[0, 0] = hg[0, 0] + row_on * row_x
    hg[2, 0] = hg[2, 0] + row_on * row_z
    col_x, col_y = border_col(2, 0)
    b_col[0] = b_col[0] + col_on * col_x
    b_col[1] = b_col[1] + col_on * col_y

    tiles_out[0] = zd_r[DOWN_AT[2]]
    tiles_out[1] = zd_r[DOWN_AT[2] + 1]
    for k in range(3):
        finish(k)
    others.wait_recv()
    whole_out[...] = jnp.sum(part[...], axis=0)
    others.wait_send()


def last_kernel(
    scale,
    cc, hg, eg, pg, qg, ng, cg, tiles_in, b_col, whole,
    eg_out, hg_out, pg_out, qg_out, ng_out, cg_out, tg_out,
    hg_v, eg_v,
    sem, row_sem,
):
    rows, depth, width = cg.shape
    tools = Shifts(depth, width)
    group = math.gcd(rows, ROWS_PER_STEP)
    chunk = math.gcd(rows, 2 * group)
    size = group * depth
    ready = ((pg, pg_out), (qg, qg_out), (ng, ng_out), (cg, cg_out))
    copies = [pltpu.make_async_copy(a, b, sem.at[i]) for i, (a, b) in enumerate(ready)]
    for copy in copies:
        copy.start()
    hg_v[0, 0] = hg[0, 0]
    hg_v[2, 0] = hg[2, 0]

    def pass_rows(i, base):
        r = base + i * group
        curl = tools.curl_forward(cc, tiles_in[0], tiles_in[1], r, group)
        out = [
            hg[c, pl.ds(r + 1, group)].reshape(size, width) + curl[c] for c in range(3)
        ]
        back = tools.curl_backward(out, hg_v[0, r], hg_v[2, r], b_col, r)
        for c in range(3):
            hg_v[c, pl.ds(r + 1, group)] = out[c].reshape(group, depth, width)
            value = eg[c, pl.ds(r, group)].reshape(size, width) - MAGNETIC_STEP * back[c]
            eg_v[c, pl.ds(r, group)] = value.reshape(group, depth, width)
        return base

    for n, base in enumerate(range(0, rows, chunk)):
        lax.fori_loop(0, chunk // group, pass_rows, base)
        part = pl.ds(base, chunk)
        for i, (a, b) in enumerate(
            ((hg_v.at[:, pl.ds(base + 1, chunk)], hg_out.at[:, part]), (eg_v.at[:, part], eg_out.at[:, part]))
        ):
            copy = pltpu.make_async_copy(a, b, row_sem.at[n, i])
            copy.start()
            copies.append(copy)
    for label in range(tg_out.shape[0]):
        tg_out[label] = jnp.sum(whole[label : label + 1, :]) * scale
    for copy in copies:
        copy.wait()


def solution(mesh):
    ngy, ngz = mesh.shape["gy"], mesh.shape["gz"]

    def on_device(*arrays):
        shape = arrays[0].shape
        _, rows, depth, width = shape
        count = arrays[12].shape[0]
        cells = rows * depth * width * ngy * ngz
        f32 = jnp.float32
        space = pl.BlockSpec(memory_space=pl.ANY)
        scalar = pl.BlockSpec(memory_space=pltpu.SMEM)
        three = jax.ShapeDtypeStruct(shape, f32)
        two = jax.ShapeDtypeStruct((2,) + shape[1:], f32)
        one = jax.ShapeDtypeStruct(shape[1:], f32)

        def vm(lead, wide=width):
            return pltpu.VMEM((lead, depth, wide), f32)

        def field(n, extra=0):
            return pltpu.VMEM((n, rows + extra, depth, width), f32)

        inputs = [
            pltpu.VMEM(arrays[i].shape, arrays[i].dtype) for i in (0, 1, 2, 3, 4, 5, 6, 7, 8, 9, 10, 11, 13)
        ]
        slots = -(-count // 8) * 8
        up, down, diag = sum(UP), sum(DOWN), sum(FIELDS)
        dma = pltpu.SemaphoreType.DMA
        scratch = inputs + [
            field(3, 1), field(3, 1), field(3, 1), field(3, 1),
            field(3), field(3), field(3), pltpu.VMEM(shape[1:], f32),
            vm(2, LANES),
            vm(up), vm(up), vm(down), vm(down),
            vm(up, LANES), vm(up, LANES), vm(down, LANES), vm(down, LANES),
            vm(diag, LANES), vm(diag, LANES),
            vm(count),
            pltpu.VMEM((ngy * ngz, slots, LANES), f32),
            dma((13,)), dma((3, 6)), dma((3, 6)), dma((2,)),
        ]
        moved = 4 * rows * depth * width * 40
        kept = pl.BlockSpec(memory_space=pltpu.VMEM)
        values = pl.pallas_call(
            functools.partial(kernel, ngy, ngz, count),
            out_shape=(
                field(3, 1), field(3, 1), field(3), field(3), field(3), field(2),
                pltpu.VMEM(shape[1:], f32), vm(2, LANES), vm(2, LANES),
                pltpu.VMEM((slots, LANES), f32),
            ),
            in_specs=[scalar if i in (12, 14) else space for i in range(15)],
            out_specs=(kept,) * 10,
            scratch_shapes=scratch,
            cost_estimate=pl.CostEstimate(
                flops=500 * rows * depth * width, bytes_accessed=moved, transcendentals=0
            ),
            compiler_params=pltpu.CompilerParams(
                collective_id=0, has_side_effects=True, vmem_limit_bytes=58 * 1024 * 1024
            ),
        )(*arrays)
        group = math.gcd(rows, ROWS_PER_STEP)
        table = jax.ShapeDtypeStruct((count,), f32)
        return pl.pallas_call(
            functools.partial(last_kernel, 1.0 / math.sqrt(cells)),
            out_shape=(three, three, three, three, two, one, table),
            in_specs=[kept] * 10,
            out_specs=(space,) * 6 + (scalar,),
            scratch_shapes=[
                field(3, 1), field(3), dma((4,)), dma((rows // math.gcd(rows, 2 * group), 2)),
            ],
            compiler_params=pltpu.CompilerParams(vmem_limit_bytes=24 * 1024 * 1024),
        )(*values)

    field = P(None, "gy", None, "gz")
    cell = P("gy", None, "gz")
    return jax.shard_map(
        on_device,
        mesh=mesh,
        in_specs=(field,) * 10 + (cell, cell, P(), cell, P()),
        out_specs=(field,) * 5 + (cell, P()),
        check_vma=False,
    )
```
